256 devices in a mesh: wide: 32 (over y, x, core), narrow: 8 (over z).
Axes of the slice: x: 4, y: 4, z: 8, core: 2. Of those that a mesh axis runs over, the one named last changes fastest.
Arguments:
- leaf_rhs: bfloat16 [131072, 256], P(('wide', 'narrow')), may hold values from -6 to 6
- leaf_inv: bfloat16 [1024, 128, 128], P(('wide', 'narrow')), may hold values from -0.5 to 0.5
- leaf_coupling: bfloat16 [1024, 2, 128, 128], P(('wide', 'narrow')), may hold values from -0.25 to 0.25
- leaf_parent: int32 [1024, 2], P(('wide', 'narrow')), may hold values from 0 to 15, all different within a row
- sep_rhs: bfloat16 [65536, 256], P(('wide', 'narrow')), may hold values from -6 to 6
- sep_inv: bfloat16 [65536, 2048], P(('wide', 'narrow')), may hold values from -0.125 to 0.125
- sep_link: bfloat16 [4096, 128], P('wide'), may hold values from -2 to 2
- row_owner: int32 [32, 8], P('wide'), may hold values from 0 to 7, each once within a row
Outputs:
- leaf_adjoint: float32 [131072, 256], P(('wide', 'narrow'))
- sep_adjoint: float32 [65536, 256], P(('wide', 'narrow'))
The draws below stay inside these ranges and needn't reach their ends.
Inputs may be any that keep to these rules, and one draw needn't show every extreme that they name: `leaf_parent`: each row names 2 different block rows of the leaf's own separator. `row_owner`: each row is a permutation of the narrow indices.
All inputs are finite; a program needn't handle non-finite values.
Results may differ from the reference program's by a relative error of at most 0.015.
Values may be sent and summed in bfloat16 or wider, within the bound.
No kernel may reach another device: no remote copies, remote signals or barrier semaphores. Data moves between devices by JAX's collectives and lax.ppermute only.
A program may use at most 64 MiB of HBM per device.

```python
import jax
import jax.numpy as jnp
from jax import lax

B = 128
K = 256
CPL = 2
LEAF_DEV = 4
SEP_DEV = 2
SUBTREES = 32
SUB_LEAVES = 32
LEAVES = 1024
GROUP = 256
SEP_BLOCKS = 16
SEP_ROWS = 2048
ALL_SEP_ROWS = 65536
N_NARROW = 8


def shard_levels(key, dims, split, smallest, largest):
    def one(axis_at, shards_of):
        heights = jax.random.uniform(jax.random.fold_in(jax.random.fold_in(key, 6), axis_at), (shards_of,), jnp.float32, smallest / len(split), largest / len(split))
        return jnp.repeat(jnp.exp(heights), dims[axis_at] // shards_of).reshape((-1,) + (1,) * (len(dims) - axis_at - 1))

    factor_of = one(*split[0])
    for cut in split[1:]:
        factor_of = factor_of * one(*cut)
    return factor_of


def distinct(rng, rows, number_of, top, lift):
    sequence = jax.random.permutation(jax.random.fold_in(rng, 1), number_of)
    pull = sequence
    for power in range(3):
        pull = pull * pull // number_of
    pull = pull * lift // number_of
    chance = jax.random.randint(jax.random.fold_in(rng, 2), (rows, number_of), 0, 4096) + pull
    sure = jax.random.permutation(jax.random.fold_in(rng, 3), rows)[jnp.arange(number_of) % rows]
    chance = jnp.where(jnp.arange(rows)[:, None] == sure[None, :], 1 << 14, chance)
    priority = chance * number_of + jnp.arange(number_of)
    return lax.top_k(priority.astype(jnp.int32), top)[1].astype(jnp.int32)


def bell_draw(key, shape, spread, reach, cuts=(), held_as=jnp.bfloat16):
    gain = shard_levels(key, shape, cuts, -0.22, 0.18) if cuts else 1.0
    entries = jax.random.normal(key, shape, jnp.float32) * spread * gain
    return jnp.minimum(jnp.maximum(entries, -reach), reach).astype(held_as)


def setup_inputs(seed: int = 0) -> dict:
    key_list = jax.random.split(jax.random.key(seed), 9)
    return {
        "leaf_rhs": bell_draw(key_list[0], (LEAVES * B, K), 1.0, 6.0, ((0, 256),)),
        "leaf_inv": bell_draw(key_list[1], (LEAVES, B, B), B ** -0.5, 0.5, ((0, 256),)),
        "leaf_coupling": bell_draw(key_list[2], (LEAVES, CPL, B, B), (B * LEAF_DEV * CPL // SEP_DEV) ** -0.5, 0.25, ((0, 256),)),
        "leaf_parent": distinct(key_list[3], LEAVES, SEP_BLOCKS, CPL, 2048),
        "sep_rhs": bell_draw(key_list[4], (ALL_SEP_ROWS, K), 1.0, 6.0, ((0, 256),)),
        "sep_inv": bell_draw(key_list[5], (ALL_SEP_ROWS, SEP_ROWS), SEP_ROWS ** -0.5, 0.125, ((0, 256),)),
        "sep_link": bell_draw(key_list[6], (SUBTREES * B, B), (B // (N_NARROW * SEP_DEV)) ** -0.5, 2.0, ((0, 32),)),
        "row_owner": jax.vmap(lambda own: jax.random.permutation(own, N_NARROW))(jax.random.split(key_list[7], SUBTREES)).reshape((SUBTREES, N_NARROW)).astype(jnp.int32),
    }


highest = lax.Precision.HIGHEST


def natural_order(stored, owner_row):
    return stored[owner_row].reshape((SEP_ROWS,) + stored.shape[2:])


def leaf_forward(inputs):
    leaf_rows, leaf_inverse, coupling, parent, rhs_groups, inv_groups, owner_row = inputs
    forward_leaf = jnp.einsum("iab,ibk->iak", leaf_inverse.astype(jnp.float32), leaf_rows.astype(jnp.float32), precision=highest).astype(jnp.bfloat16)
    pushed = jnp.einsum("icab,ibk->icak", coupling.astype(jnp.float32), forward_leaf.astype(jnp.float32), precision=highest)
    selector = (parent[:, :, None] == jnp.arange(SEP_BLOCKS, dtype=jnp.int32)[None, None, :]).astype(jnp.float32)
    summed = jnp.einsum("icn,icak->nak", selector, pushed, precision=highest).reshape(SEP_ROWS, K)
    coupled = (natural_order(rhs_groups, owner_row).astype(jnp.float32) - summed).astype(jnp.bfloat16)
    applied = jnp.dot(natural_order(inv_groups, owner_row), coupled, preferred_element_type=jnp.float32)
    return forward_leaf, applied


def forward_chain(state, inputs):
    applied, inv_groups, owner_row, link_block = inputs
    head_cols = natural_order(inv_groups, owner_row)[:, :B].astype(jnp.float32)
    moved = jnp.dot(link_block.astype(jnp.float32), state, precision=highest)
    result = applied - jnp.dot(head_cols, moved, precision=highest)
    return result[SEP_ROWS - B:], result.astype(jnp.bfloat16)


def adjoint_chain(incoming, inputs):
    inv_groups, owner_row, rounded, link_block = inputs
    natural_inv = natural_order(inv_groups, owner_row)
    head_part = jnp.einsum("ab,ak->bk", natural_inv[:, :B].astype(jnp.float32), rounded.astype(jnp.float32), precision=highest)
    tail_block = natural_inv[SEP_ROWS - B:, :B].astype(jnp.float32)
    passed = head_part - jnp.dot(tail_block.T, incoming, precision=highest)
    return jnp.dot(link_block.astype(jnp.float32).T, passed, precision=highest), incoming


def separator_adjoint(inputs):
    inv_groups, owner_row, rounded, incoming = inputs
    natural_inv = natural_order(inv_groups, owner_row)
    adjusted = (rounded.astype(jnp.float32) - jnp.pad(incoming, ((SEP_ROWS - B, 0), (0, 0)))).astype(jnp.bfloat16)
    result = jnp.einsum("ab,ak->bk", natural_inv.astype(jnp.float32), adjusted.astype(jnp.float32), precision=highest)
    inverse = jnp.argsort(owner_row).astype(jnp.int32)
    stored = result.reshape(N_NARROW, GROUP, K)[inverse]
    return result, stored


def leaf_backward(inputs):
    leaf_inverse, coupling, parent, forward_leaf, natural_sep = inputs
    rounded = natural_sep.astype(jnp.bfloat16).reshape(SEP_BLOCKS, B, K)
    chosen = rounded[parent]
    pulled = jnp.einsum("icab,icak->ibk", coupling.astype(jnp.float32), chosen.astype(jnp.float32), precision=highest)
    middle = (forward_leaf.astype(jnp.float32) - pulled).astype(jnp.bfloat16)
    return jnp.einsum("iab,iak->ibk", leaf_inverse.astype(jnp.float32), middle.astype(jnp.float32), precision=highest)


def reference(leaf_rhs, leaf_inv, leaf_coupling, leaf_parent, sep_rhs, sep_inv, sep_link, row_owner):
    leaf_rows = leaf_rhs.reshape(SUBTREES, SUB_LEAVES, B, K)
    leaf_inverse = leaf_inv.reshape(SUBTREES, SUB_LEAVES, B, B)
    coupling = leaf_coupling.reshape(SUBTREES, SUB_LEAVES, CPL, B, B)
    parent = leaf_parent.reshape(SUBTREES, SUB_LEAVES, CPL)
    rhs_groups = sep_rhs.reshape(SUBTREES, N_NARROW, GROUP, K)
    inv_groups = sep_inv.reshape(SUBTREES, N_NARROW, GROUP, SEP_ROWS)
    links = sep_link.reshape(SUBTREES, B, B)
    forward_leaf, applied = lax.map(leaf_forward, (leaf_rows, leaf_inverse, coupling, parent, rhs_groups, inv_groups, row_owner))
    start_state = jnp.zeros((B, K), jnp.float32)
    ending, forward_round = lax.scan(forward_chain, start_state, (applied, inv_groups, row_owner, links))
    ending, incoming = lax.scan(adjoint_chain, start_state, (inv_groups, row_owner, forward_round, links), reverse=True)
    natural_sep, stored_sep = lax.map(separator_adjoint, (inv_groups, row_owner, forward_round, incoming))
    leaf_result = lax.map(leaf_backward, (leaf_inverse, coupling, parent, forward_leaf, natural_sep))
    return leaf_result.reshape(LEAVES * B, K), stored_sep.reshape(ALL_SEP_ROWS, K)
```

```python
import jax
import jax.numpy as jnp
from jax import lax
from jax.experimental import pallas as pl
from jax.experimental.pallas import tpu as pltpu
from jax.sharding import PartitionSpec as P

BF = jnp.bfloat16
F32 = jnp.float32
VMEM = pl.BlockSpec(memory_space=pltpu.VMEM)
SMEM = pl.BlockSpec(memory_space=pltpu.SMEM)
LIMIT = 56 * 1024 * 1024

NN = (((1,), (0,)), ((), ()))
NT = (((1,), (1,)), ((), ()))
TN = (((0,), (0,)), ((), ()))


def mm(a, b, dims):
    return lax.dot_general(a, b, dims, preferred_element_type=F32)


def halves(v):
    hi = v.astype(BF)
    return hi, (v - hi.astype(F32)).astype(BF)


def mm3(a, b, dims):
    ah, al = halves(a)
    bh, bl = halves(b)
    return mm(ah, bh, dims) + (mm(al, bh, dims) + mm(ah, bl, dims))


def mm2(a, b_exact, dims):
    ah = a.astype(BF)
    rest = a - ah.astype(F32)
    al = rest.astype(BF)
    ax = (rest - al.astype(F32)).astype(BF)
    return mm(ah, b_exact, dims) + (mm(al, b_exact, dims) + mm(ax, b_exact, dims))


def call(kernel, name, outs, n_smem, n_vmem, scratch=(), flops=0, moved=0):
    return pl.pallas_call(
        kernel,
        name=name,
        out_shape=outs,
        in_specs=[SMEM] * n_smem + [VMEM] * n_vmem,
        out_specs=jax.tree.map(lambda _: VMEM, outs),
        scratch_shapes=list(scratch),
        compiler_params=pltpu.CompilerParams(vmem_limit_bytes=LIMIT),
        cost_estimate=pl.CostEstimate(flops=flops, bytes_accessed=moved, transcendentals=0),
    )


def leaf_forward_kernel(parent, group, rhs, inv, cpl, sep_rhs, fl, local, acc):
    b = inv.shape[1]
    rows = sep_rhs.shape[0]
    acc[...] = jnp.zeros_like(acc)
    start = pl.multiple_of(group[0] * rows, rows)
    acc[pl.ds(start, rows), :] = sep_rhs[...].astype(F32)
    for i in range(inv.shape[0]):
        f = mm(inv[i], rhs[i * b : (i + 1) * b, :], NN).astype(BF)
        fl[i * b : (i + 1) * b, :] = f
        for k in range(cpl.shape[1]):
            at = pl.ds(pl.multiple_of(parent[i, k] * b, b), b)
            acc[at, :] -= mm(cpl[i, k], f, NN)
    local[...] = acc[...].astype(BF)


def sum_spread_kernel(parts, spread):
    total = parts[0].astype(F32)
    for j in range(1, parts.shape[0]):
        total += parts[j].astype(F32)
    total = total.astype(BF)
    for j in range(parts.shape[0]):
        spread[j] = total


def sum_keep_spread_kernel(parts, kept, spread):
    total = parts[0].astype(F32)
    for j in range(1, parts.shape[0]):
        total += parts[j].astype(F32)
    kept[...] = total
    total = total.astype(BF)
    for j in range(parts.shape[0]):
        spread[j] = total


def middle_kernel(owners, last, inv, coupled, ag, terms):
    rows = inv.shape[0]
    b = rows // 2
    applied = mm(inv[...], coupled[...], NN)
    app = applied.astype(BF)
    ag[:, :b] = jnp.where(last[0] == 1, applied[rows - b :, :].T, 0.0)
    ag[:, b:] = mm(app, inv[:, :b], TN)
    for g in range(terms.shape[0]):
        terms[owners[g]] = mm(inv[:, g * rows : (g + 1) * rows], app, TN).astype(BF)


def small_sum_kernel(parts, link, spread):
    b = link.shape[0]
    total = parts[0]
    for j in range(1, parts.shape[0]):
        total += parts[j]
    moved = mm2(total[:, b:], link[...], NN)
    for j in range(spread.shape[0]):
        spread[j, :, :b] = total[:, :b]
        spread[j, :, b:] = moved


def maps_kernel(x, link, out):
    b = link.shape[0]
    corner = x[:, :b]
    tail = x[:, b:].astype(BF)
    out[:b, :] = mm(link[...], tail, (((0,), (1,)), ((), ())))
    out[b : 2 * b, :] = mm(tail, link[...], NN)
    inner = mm2(corner, link[...], NN)
    out[2 * b :, :] = mm2(inner, link[...], TN)


def chain_kernel(core, me, ag_own, ag_other, maps, link, out, ag, states, incoming):
    b = link.shape[0]
    length = maps.shape[0]
    here = core[0]
    pairs = length // 2
    ag[here] = ag_own[...]
    ag[1 - here] = ag_other[...]
    state = jnp.zeros((ag_own.shape[1], b), F32)
    for w in range(length):
        states[w] = state
        if w + 1 < length:
            state = ag[w % 2, w // 2, :, :b] - mm3(state, maps[w, :b, :], NN)
    back = jnp.zeros_like(state)
    for w in range(length - 1, -1, -1):
        incoming[w] = back
        if w > 0:
            local = ag[w % 2, w // 2, :, b:] - mm3(states[w], maps[w, 2 * b :, :], NN)
            back = local - mm3(back, maps[w, b : 2 * b, :], NN)
    mine = mm2(states[me[0]], link[...], NT)
    for j in range(out.shape[0]):
        out[j, :, :b] = mine
        out[j, :, b:] = incoming[me[0]]


def final_kernel(
    parent, owners, group, kept, gathered, shared, z, cpl, inv, fl, leaf_out, sep_out, zs
):
    b = inv.shape[1]
    rows = kept.shape[0]
    zh, zl = halves(z[...])
    zs[0] = zh
    zs[1] = zl

    def fix(start, count):
        part = shared[pl.ds(start, count), :]
        ph, pw = halves(part)
        return mm(ph, zs[0], NT) + (mm(pw, zs[0], NT) + mm(ph, zs[1], NT))

    at = pl.multiple_of(group[0] * rows, rows)
    sep_out[...] = kept[...] - fix(at, rows)
    for i in range(inv.shape[0]):
        acc = fl[i * b : (i + 1) * b, :].astype(F32)
        for k in range(cpl.shape[1]):
            p = parent[i, k]
            half = lax.rem(p, 2)
            stored = pl.multiple_of(owners[lax.div(p, 2)] * rows + half * b, b)
            block = gathered[pl.ds(stored, b), :].astype(F32)
            block = (block - fix(pl.multiple_of(p * b, b), b)).astype(BF)
            acc -= mm(cpl[i, k], block, TN)
        leaf_out[i * b : (i + 1) * b, :] = mm(inv[i], acc.astype(BF), TN)


def swap(value, axis, by):
    n = lax.axis_size(axis)
    return lax.ppermute(value, axis, [(i, i ^ by) for i in range(n)])


def per_device(
    leaf_rhs, leaf_inv, leaf_coupling, leaf_parent, sep_rhs, sep_inv, sep_link, row_owner
):
    b = leaf_inv.shape[1]
    leaf_count = leaf_inv.shape[0]
    sketch = leaf_rhs.shape[1]
    rows = sep_inv.shape[0]
    n = lax.axis_size("narrow")
    chain_len = lax.axis_size("wide")
    all_rows = sep_inv.shape[1]
    cols = sketch // n
    narrow = lax.axis_index("narrow")
    wide = lax.axis_index("wide")
    owners = row_owner[0]
    ids = jnp.arange(n, dtype=jnp.int32)
    group = jnp.sum(jnp.where(owners == narrow, ids, 0)).reshape(1)
    last = (owners[n - 1] == narrow).astype(jnp.int32).reshape(1)
    is_last = last[0] == 1
    shape = jax.ShapeDtypeStruct

    head = sep_inv[:, :b]
    corner = mm(head, head, TN)
    tail = jnp.where(is_last, head[rows - b :], jnp.zeros((), BF)).astype(F32)
    x = jnp.concatenate([corner, tail], axis=1)
    for by in (1, 2, 4):
        x = x + swap(x, "narrow", by)
    maps = call(maps_kernel, "maps", shape((3 * b, b), F32), 0, 2, flops=2 * 9 * b**3)(x, sep_link)
    maps = lax.all_gather(maps, "wide", axis=0, tiled=False)
    rows_at = lax.broadcasted_iota(jnp.int32, (rows, b), 0)
    cols_at = lax.broadcasted_iota(jnp.int32, (rows, b), 1)
    pick = jnp.where(is_last & (rows_at == cols_at + (rows - b)), 1.0, 0.0).astype(BF)
    shared = lax.psum(mm(sep_inv, jnp.concatenate([head, pick], axis=1), TN), "narrow")

    fl, local = call(
        leaf_forward_kernel,
        "leaf_forward",
        (shape((leaf_count * b, sketch), BF), shape((all_rows, sketch), BF)),
        2,
        4,
        [pltpu.VMEM((all_rows, sketch), F32)],
        flops=2 * 12 * b * b * sketch,
        moved=4 << 20,
    )(leaf_parent, group, leaf_rhs, leaf_inv, leaf_coupling, sep_rhs)
    parts = lax.all_to_all(local.reshape(n, rows, sketch), "narrow", 0, 0, tiled=True)
    spread = call(
        sum_spread_kernel, "sum_spread", shape((n, rows, sketch), BF), 0, 1, moved=2 << 20
    )(parts)
    coupled = lax.all_to_all(spread, "narrow", 0, 0, tiled=True).reshape(all_rows, sketch)
    ag, terms = call(
        middle_kernel,
        "middle",
        (shape((sketch, 2 * b), F32), shape((n, rows, sketch), BF)),
        2,
        2,
        flops=4 * rows * all_rows * sketch,
        moved=4 << 20,
    )(owners, last, sep_inv, coupled)

    ag = lax.all_to_all(ag.reshape(n, cols, 2 * b), "narrow", 0, 0, tiled=True)
    quad = 4
    ag = call(
        small_sum_kernel, "small_sum", shape((quad, cols, 2 * b), F32), 0, 2, moved=1 << 19
    )(ag, sep_link)
    x_groups = [[y * 8 + i * 2 + c for i in range(4)] for y in range(4) for c in range(2)]
    y_groups = [[i * 8 + xx * 2 + c for i in range(4)] for xx in range(4) for c in range(2)]
    ag = lax.all_to_all(ag, "wide", 0, 0, tiled=True, axis_index_groups=x_groups)
    ag = jnp.broadcast_to(ag[None], (quad,) + ag.shape)
    ag = lax.all_to_all(ag, "wide", 0, 0, tiled=True, axis_index_groups=y_groups)
    ag = ag.reshape(quad * quad, cols, 2 * b)
    other = swap(ag, "wide", 1)
    core = lax.rem(wide, 2).astype(jnp.int32).reshape(1)
    z = call(
        chain_kernel,
        "chain",
        shape((n, cols, 2 * b), F32),
        2,
        4,
        [
            pltpu.VMEM((2, chain_len // 2, cols, 2 * b), F32),
            pltpu.VMEM((chain_len, cols, b), F32),
            pltpu.VMEM((chain_len, cols, b), F32),
        ],
        flops=2 * 9 * chain_len * cols * b * b * 40,
        moved=8 << 20,
    )(core, wide.astype(jnp.int32).reshape(1), ag, other, maps, sep_link)
    z = lax.all_to_all(z, "narrow", 0, 0, tiled=True).reshape(sketch, 2 * b)

    terms = lax.all_to_all(terms, "narrow", 0, 0, tiled=True)
    kept, spread = call(
        sum_keep_spread_kernel,
        "sum_keep_spread",
        (shape((rows, sketch), F32), shape((n, rows, sketch), BF)),
        0,
        1,
        moved=2 << 20,
    )(terms)
    gathered = lax.all_to_all(spread, "narrow", 0, 0, tiled=True).reshape(all_rows, sketch)

    leaf_out, sep_out = call(
        final_kernel,
        "final",
        (shape((leaf_count * b, sketch), F32), shape((rows, sketch), F32)),
        3,
        7,
        [pltpu.VMEM((2, sketch, 2 * b), BF)],
        flops=2 * 40 * b * b * sketch,
        moved=6 << 20,
    )(leaf_parent, owners, group, kept, gathered, shared, z, leaf_coupling, leaf_inv, fl)
    return leaf_out, sep_out


def solution(mesh):
    both = ("wide", "narrow")
    placed = (
        P(both, None),
        P(both, None, None),
        P(both, None, None, None),
        P(both, None),
        P(both, None),
        P(both, None),
        P("wide", None),
        P("wide", None),
    )
    return jax.shard_map(
        per_device,
        mesh=mesh,
        in_specs=placed,
        out_specs=(P(both, None), P(both, None)),
        check_vma=False,
    )
```

```python
import jax
import jax.numpy as jnp
from jax import lax
from jax.experimental import pallas as pl
from jax.experimental.pallas import tpu as pltpu
from jax.sharding import PartitionSpec as P

BF = jnp.bfloat16
F32 = jnp.float32
VMEM = pl.BlockSpec(memory_space=pltpu.VMEM)
SMEM = pl.BlockSpec(memory_space=pltpu.SMEM)
ANY = pl.BlockSpec(memory_space=pl.ANY)
LIMIT = 56 * 1024 * 1024

NN = (((1,), (0,)), ((), ()))
NT = (((1,), (1,)), ((), ()))
TN = (((0,), (0,)), ((), ()))


def mm(a, b, dims):
    return lax.dot_general(a, b, dims, preferred_element_type=F32)


def halves(v):
    hi = v.astype(BF)
    return hi, (v - hi.astype(F32)).astype(BF)


def mm3(a, b, dims):
    ah, al = halves(a)
    bh, bl = halves(b)
    return mm(ah, bh, dims) + (mm(al, bh, dims) + mm(ah, bl, dims))


def mm2(a, b_exact, dims):
    ah = a.astype(BF)
    rest = a - ah.astype(F32)
    al = rest.astype(BF)
    ax = (rest - al.astype(F32)).astype(BF)
    return mm(ah, b_exact, dims) + (mm(al, b_exact, dims) + mm(ax, b_exact, dims))


def call(kernel, name, outs, ins, scratch=(), flops=0, moved=0):
    return pl.pallas_call(
        kernel,
        name=name,
        out_shape=outs,
        in_specs=ins,
        out_specs=jax.tree.map(lambda _: VMEM, outs, is_leaf=lambda o: hasattr(o, "dtype")),
        scratch_shapes=list(scratch),
        compiler_params=pltpu.CompilerParams(vmem_limit_bytes=LIMIT),
        cost_estimate=pl.CostEstimate(flops=flops, bytes_accessed=moved, transcendentals=0),
    )


def held_group(owners):
    me = lax.axis_index("narrow")
    group = jnp.int32(0)
    for g in range(1, 8):
        group = jnp.where(owners[0, g] == me, g, group)
    return group


def leaf_forward_kernel(parent, owners, rhs, inv, cpl, sep_rhs, sep_inv, fl, *refs):
    blocks = refs[:-3]
    acc, head, sem = refs[-3:]
    fetch = pltpu.make_async_copy(sep_inv.at[:, pl.ds(0, head.shape[1])], head, sem)
    fetch.start()
    b = inv.shape[1]
    rows = sep_rhs.shape[0]
    n = len(blocks)
    me = lax.axis_index("narrow")
    acc[...] = jnp.zeros_like(acc)
    start = pl.multiple_of(held_group(owners) * rows, rows)
    acc[pl.ds(start, rows), :] = sep_rhs[...].astype(F32)
    for i in range(inv.shape[0]):
        f = mm(inv[i], rhs[i * b : (i + 1) * b, :], NN).astype(BF)
        fl[i * b : (i + 1) * b, :] = f
        for k in range(cpl.shape[1]):
            at = pl.ds(pl.multiple_of(parent[k, i] * b, b), b)
            acc[at, :] -= mm(cpl[i, k], f, NN)
    fetch.wait()
    corner_hi, corner_lo = halves(mm(head[...], head[...], TN))
    acc[n * rows : n * rows + b, :b] = corner_hi.astype(F32)
    acc[n * rows : n * rows + b, b:] = corner_lo.astype(F32)
    tail = head[rows - b :, :].astype(F32)
    acc[n * rows + b :, :b] = jnp.where(owners[0, n - 1] == me, tail, 0.0)
    step = b // n
    for j in range(n):
        g = lax.rem(me + j, n)
        blocks[j][:rows, :] = acc[pl.ds(pl.multiple_of(g * rows, rows), rows), :].astype(BF)
        corner = acc[pl.ds(pl.multiple_of(n * rows + g * step, step), step), :].astype(BF)
        tail = acc[pl.ds(pl.multiple_of(n * rows + b + g * step, step), step), :b].astype(BF)
        blocks[j][rows : rows + step, :b] = tail
        blocks[j][rows : rows + step, b:] = corner[:, :b]
        blocks[j][rows + step :, :b] = corner[:, b:]
        blocks[j][rows + step :, b:] = corner[:, b:]


def sum_own_kernel(right, left, local, out):
    rows = right.shape[1]
    b = rows // 2
    step = (right.shape[0] - rows) // 2
    total = right[...].astype(F32) + left[...].astype(F32) + local[...].astype(F32)
    corner_hi, corner_lo = halves(total[rows : rows + step, b:] + total[rows + step :, :b])
    out[:rows, :] = total[:rows].astype(BF)
    out[rows : rows + step, :b] = total[rows : rows + step, :b].astype(BF)
    out[rows : rows + step, b:] = corner_hi
    out[rows + step :, :b] = corner_lo
    out[rows + step :, b:] = corner_lo


def pack_kernel(kept, shared, *refs):
    packed = refs[-1]
    rows = kept.shape[0]
    packed[:rows, :] = kept[...]
    packed[rows:, :] = shared[...]


def middle_kernel(owners, inv, *refs):
    n = 8
    coupled = refs[:n]
    link, _, ag, terms, maps, whole, corner, tail = refs[n:]
    me = lax.axis_index("narrow")
    rows = inv.shape[0]
    b = rows // 2
    step = b // n
    for j in range(n):
        g = lax.rem(me + j, n)
        block = coupled[j]
        whole[pl.ds(pl.multiple_of(g * rows, rows), rows), :] = block[:rows, :]
        at = pl.ds(pl.multiple_of(g * step, step), step)
        tail[at, :] = block[rows : rows + step, :b]
        corner[at, :] = block[rows : rows + step, b:].astype(F32) + block[
            rows + step :, :b
        ].astype(F32)
    applied = mm(inv[...], whole[...], NN)
    app = applied.astype(BF)
    for g in range(n):
        terms[owners[0, g]] = mm(inv[:, g * rows : (g + 1) * rows], app, TN).astype(BF)
    ag[:, :b] = jnp.where(owners[0, n - 1] == me, applied[rows - b :, :], 0.0).T
    ag[:, b:] = mm(app, inv[:, :b], TN)
    maps[:b, :] = mm(tail[...], link[...], NN)
    inner = mm2(corner[...], link[...], NN)
    maps[b:, :] = mm2(inner, link[...], TN)


def small_sum_kernel(parts, link, _, spread):
    b = link.shape[0]
    total = parts[0]
    for j in range(1, parts.shape[0]):
        total += parts[j]
    moved = mm2(total[:, b:], link[...], NN)
    for j in range(spread.shape[0]):
        spread[j, :, :b] = total[:, :b]
        spread[j, :, b:] = moved


def chain_kernel(*refs):
    ag_own, ag_other = refs[:2]
    maps_own, maps_other = refs[2:6], refs[6:10]
    link, out, ag, maps, states, incoming, sems = refs[11:]
    b = link.shape[0]
    length = states.shape[0]
    wide = lax.axis_index("wide")
    here = lax.rem(wide, 2)
    x = lax.rem(lax.div(wide, 2), 4)
    y = lax.div(wide, 8)
    copies = []
    for side, ag_part, parts in ((here, ag_own, maps_own), (1 - here, ag_other, maps_other)):
        copies.append((ag_part, ag.at[side]))
        for j in range(4):
            for k in range(4):
                at = lax.rem(y + j, 4) * 4 + lax.rem(x + k, 4)
                copies.append((parts[j].at[k], maps.at[side, at]))
    copies = [pltpu.make_async_copy(p, q, sems.at[i]) for i, (p, q) in enumerate(copies)]
    for copy in copies:
        copy.start()
    for copy in copies:
        copy.wait()
    state = jnp.zeros((out.shape[1], b), F32)
    for w in range(length):
        states[w] = state
        if w + 1 < length:
            state = ag[w % 2, w // 2, :, :b] - mm3(state, maps[w % 2, w // 2, :b, :], NT)
    back = jnp.zeros_like(state)
    for w in range(length - 1, -1, -1):
        incoming[w] = back
        if w > 0:
            local = ag[w % 2, w // 2, :, b:] - mm3(states[w], maps[w % 2, w // 2, b:, :], NN)
            back = local - mm3(back, maps[w % 2, w // 2, :b, :], NN)
    mine = mm2(states[wide], link[...], NT)
    for j in range(out.shape[0]):
        out[j, :, :b] = mine
        out[j, :, b:] = incoming[wide]


def final_kernel(
    parent, owners, kept, gathered, z, cpl, inv, fl, leaf_out, sep_out, zs
):
    b = inv.shape[1]
    rows = kept.shape[0]
    zh, zl = halves(z[...])
    zs[0] = zh
    zs[1] = zl

    def fix(g, start, count):
        part = gathered[g, pl.ds(rows + start, count), :]
        return mm(part, zs[0], NT) + mm(part, zs[1], NT)

    sep_out[...] = kept[...].astype(F32) - fix(held_group(owners), 0, rows)
    for i in range(inv.shape[0]):
        acc = fl[i * b : (i + 1) * b, :].astype(F32)
        for k in range(cpl.shape[1]):
            p = parent[k, i]
            g = lax.div(p, 2)
            at = pl.multiple_of(lax.rem(p, 2) * b, b)
            block = gathered[owners[0, g], pl.ds(at, b), :].astype(F32)
            block = (block - fix(g, at, b)).astype(BF)
            acc -= mm(cpl[i, k], block, TN)
        leaf_out[i * b : (i + 1) * b, :] = mm(inv[i], acc.astype(BF), TN)


def swap(value, axis, by):
    n = lax.axis_size(axis)
    return lax.ppermute(value, axis, [(i, i ^ by) for i in range(n)])


def turned(value, by):
    n = lax.axis_size("narrow")
    return lax.ppermute(value, "narrow", [(i, (i + by) % n) for i in range(n)])


def ring_sum(blocks):
    def plus(value, block):
        return (value.astype(F32) + block.astype(F32)).astype(BF)

    right = turned(blocks[4], 1)
    left = turned(blocks[5], -1)
    right = turned(plus(right, blocks[3]), 1)
    left = turned(plus(left, blocks[6]), -1)
    right = turned(plus(right, blocks[2]), 1)
    left = turned(plus(left, blocks[7]), -1)
    right = turned(plus(right, blocks[1]), 1)
    return right, left


def ring_gather(block):
    ahead = [block]
    behind = [block]
    for _ in range(3):
        behind.append(turned(behind[-1], 1))
        ahead.append(turned(ahead[-1], -1))
    behind.append(turned(behind[-1], 1))
    return ahead + behind[:0:-1]


def turned_wide(value, along, by):
    def source(i):
        y, x, core = i // 8, (i // 2) % 4, i % 2
        y, x = (y, (x + by) % 4) if along == "x" else ((y + by) % 4, x)
        return (y * 4 + x) * 2 + core

    return lax.ppermute(value, "wide", [(source(i), i) for i in range(32)])


def per_device(
    leaf_rhs, leaf_inv, leaf_coupling, leaf_parent, sep_rhs, sep_inv, sep_link, row_owner
):
    b = leaf_inv.shape[1]
    leaf_count = leaf_inv.shape[0]
    sketch = leaf_rhs.shape[1]
    rows = sep_inv.shape[0]
    n = lax.axis_size("narrow")
    chain_len = lax.axis_size("wide")
    chips = chain_len // 2
    all_rows = sep_inv.shape[1]
    cols = sketch // n
    parent = leaf_parent.T
    shape = jax.ShapeDtypeStruct
    held = pltpu.VMEM

    extra = rows + 2 * (b // n)
    fl, *blocks = call(
        leaf_forward_kernel,
        "leaf_forward",
        (shape((leaf_count * b, sketch), BF),) + (held((extra, sketch), BF),) * n,
        [SMEM] * 2 + [VMEM] * 4 + [ANY],
        [
            pltpu.VMEM((all_rows + 2 * b, sketch), F32),
            pltpu.VMEM((rows, b), BF),
            pltpu.SemaphoreType.DMA,
        ],
        flops=2 * 12 * b * b * sketch,
        moved=4 << 20,
    )(parent, row_owner, leaf_rhs, leaf_inv, leaf_coupling, sep_rhs, sep_inv)
    right, left = ring_sum(blocks)
    own = call(sum_own_kernel, "sum_own", held((extra, sketch), BF), [VMEM] * 3, moved=1 << 18)(
        right, left, blocks[0]
    )
    coupled = ring_gather(own)

    rows_at = lax.broadcasted_iota(jnp.int32, (rows, b), 0)
    cols_at = lax.broadcasted_iota(jnp.int32, (rows, b), 1)
    last = row_owner[0, n - 1] == lax.axis_index("narrow")
    pick = jnp.where(last & (rows_at == cols_at + (rows - b)), 1.0, 0.0).astype(BF)
    shared = mm(sep_inv, jnp.concatenate([sep_inv[:, :b], pick], axis=1), TN).astype(BF)
    shared = lax.psum_scatter(shared, "narrow", scatter_dimension=0, tiled=True)

    ag, terms, maps = call(
        middle_kernel,
        "middle",
        (
            shape((sketch, 2 * b), F32),
            shape((n, rows, sketch), BF),
            shape((2 * b, b), F32),
        ),
        [SMEM] + [VMEM] * (2 + n) + [ANY],
        [
            pltpu.VMEM((all_rows, sketch), BF),
            pltpu.VMEM((b, b), F32),
            pltpu.VMEM((b, b), BF),
        ],
        flops=4 * rows * all_rows * sketch,
        moved=4 << 20,
    )(row_owner, sep_inv, *coupled, sep_link, shared)

    kept = lax.psum_scatter(
        terms.reshape(all_rows, sketch), "narrow", scatter_dimension=0, tiled=True
    )
    maps = jnp.stack([maps] + [turned_wide(maps, "x", k) for k in (1, 2, 3)])
    maps = [maps] + [turned_wide(maps, "y", k) for k in (1, 2, 3)]
    maps_other = [swap(part, "wide", 1) for part in maps]
    ag = lax.all_to_all(ag.reshape(n, cols, 2 * b), "narrow", 0, 0, tiled=True)
    ag = call(
        small_sum_kernel,
        "small_sum",
        shape((chips, cols, 2 * b), F32),
        [VMEM] * 2 + [ANY],
        moved=1 << 19,
    )(ag, sep_link, maps[0])
    same_core = [[2 * q + c for q in range(chips)] for c in range(2)]
    ag = lax.all_to_all(ag, "wide", 0, 0, tiled=True, axis_index_groups=same_core)
    other = swap(ag, "wide", 1)
    packed = call(
        pack_kernel, "pack", shape((2 * rows, sketch), BF), [VMEM] * 2 + [ANY] * 4, moved=1 << 19
    )(kept, shared, other, *maps[1:])
    gathered = lax.all_gather(packed, "narrow", axis=0, tiled=False)
    z = call(
        chain_kernel,
        "chain",
        shape((n, cols, 2 * b), F32),
        [ANY] * 11 + [VMEM],
        [
            pltpu.VMEM((2, chips, cols, 2 * b), F32),
            pltpu.VMEM((2, chips, 2 * b, b), F32),
            pltpu.VMEM((chain_len, cols, b), F32),
            pltpu.VMEM((chain_len, cols, b), F32),
            pltpu.SemaphoreType.DMA((2 + 2 * chips,)),
        ],
        flops=2 * 9 * chain_len * cols * b * b,
        moved=8 << 20,
    )(ag, other, *maps, *maps_other, packed, sep_link)
    z = lax.all_to_all(z, "narrow", 0, 0, tiled=True).reshape(sketch, 2 * b)

    leaf_out, sep_out = call(
        final_kernel,
        "final",
        (shape((leaf_count * b, sketch), F32), shape((rows, sketch), F32)),
        [SMEM] * 2 + [VMEM] * 6,
        [pltpu.VMEM((2, sketch, 2 * b), BF)],
        flops=2 * 40 * b * b * sketch,
        moved=6 << 20,
    )(parent, row_owner, kept, gathered, z, leaf_coupling, leaf_inv, fl)
    return leaf_out, sep_out


def solution(mesh):
    both = ("wide", "narrow")
    placed = (
        P(both, None),
        P(both, None, None),
        P(both, None, None, None),
        P(both, None),
        P(both, None),
        P(both, None),
        P("wide", None),
        P("wide", None),
    )
    return jax.shard_map(
        per_device,
        mesh=mesh,
        in_specs=placed,
        out_specs=(P(both, None), P(both, None)),
        check_vma=False,
    )
```

```python
import jax
import jax.numpy as jnp
from jax import lax
from jax.experimental import pallas as pl
from jax.experimental.pallas import tpu as pltpu
from jax.sharding import PartitionSpec as P

BF = jnp.bfloat16
F32 = jnp.float32
VMEM = pl.BlockSpec(memory_space=pltpu.VMEM)
SMEM = pl.BlockSpec(memory_space=pltpu.SMEM)
ANY = pl.BlockSpec(memory_space=pl.ANY)
LIMIT = 56 * 1024 * 1024

NN = (((1,), (0,)), ((), ()))
NT = (((1,), (1,)), ((), ()))
TN = (((0,), (0,)), ((), ()))


def mm(a, b, dims):
    return lax.dot_general(a, b, dims, preferred_element_type=F32)


def halves(v):
    hi = v.astype(BF)
    return hi, (v - hi.astype(F32)).astype(BF)


def mm3(a, b, dims):
    ah, al = halves(a)
    bh, bl = halves(b)
    return mm(ah, bh, dims) + (mm(al, bh, dims) + mm(ah, bl, dims))


def mm2(a, b_exact, dims):
    ah = a.astype(BF)
    rest = a - ah.astype(F32)
    al = rest.astype(BF)
    ax = (rest - al.astype(F32)).astype(BF)
    return mm(ah, b_exact, dims) + (mm(al, b_exact, dims) + mm(ax, b_exact, dims))


def call(kernel, name, outs, ins, scratch=(), flops=0, moved=0):
    return pl.pallas_call(
        kernel,
        name=name,
        out_shape=outs,
        in_specs=ins,
        out_specs=jax.tree.map(lambda _: VMEM, outs, is_leaf=lambda o: hasattr(o, "dtype")),
        scratch_shapes=list(scratch),
        compiler_params=pltpu.CompilerParams(vmem_limit_bytes=LIMIT),
        cost_estimate=pl.CostEstimate(flops=flops, bytes_accessed=moved, transcendentals=0),
    )


def held_group(owners):
    me = lax.axis_index("narrow")
    group = jnp.int32(0)
    for g in range(1, 8):
        group = jnp.where(owners[0, g] == me, g, group)
    return group


def leaf_forward_kernel(parent, owners, rhs, inv, cpl, sep_rhs, sep_inv, fl, shared, *refs):
    blocks = refs[:-1]
    acc = refs[-1]
    b = inv.shape[1]
    rows = sep_rhs.shape[0]
    n = len(blocks)
    me = lax.axis_index("narrow")
    acc[...] = jnp.zeros_like(acc)
    start = pl.multiple_of(held_group(owners) * rows, rows)
    acc[pl.ds(start, rows), :] = sep_rhs[...].astype(F32)
    for i in range(inv.shape[0]):
        f = mm(inv[i], rhs[i * b : (i + 1) * b, :], NN).astype(BF)
        fl[i * b : (i + 1) * b, :] = f
        for k in range(cpl.shape[1]):
            at = pl.ds(pl.multiple_of(parent[k, i] * b, b), b)
            acc[at, :] -= mm(cpl[i, k], f, NN)
    head = sep_inv[:, :b]
    corner_hi, corner_lo = halves(mm(head, head, TN))
    acc[n * rows : n * rows + b, :b] = corner_hi.astype(F32)
    acc[n * rows : n * rows + b, b:] = corner_lo.astype(F32)
    holds_last = owners[0, n - 1] == me
    acc[n * rows + b :, :b] = jnp.where(holds_last, head[rows - b :, :].astype(F32), 0.0)
    rows_at = lax.broadcasted_iota(jnp.int32, (rows, b), 0)
    cols_at = lax.broadcasted_iota(jnp.int32, (rows, b), 1)
    pick = jnp.where(holds_last & (rows_at == cols_at + (rows - b)), 1.0, 0.0).astype(BF)
    ends = jnp.concatenate([head, pick], axis=1)
    for g in range(n):
        at = slice(g * rows, (g + 1) * rows)
        shared[at, :] = mm(sep_inv[:, at], ends, TN).astype(BF)
    step = b // n
    for j in range(n):
        g = lax.rem(me + j, n)
        blocks[j][:rows, :] = acc[pl.ds(pl.multiple_of(g * rows, rows), rows), :].astype(BF)
        corner = acc[pl.ds(pl.multiple_of(n * rows + g * step, step), step), :].astype(BF)
        tail = acc[pl.ds(pl.multiple_of(n * rows + b + g * step, step), step), :b].astype(BF)
        blocks[j][rows : rows + step, :b] = tail
        blocks[j][rows : rows + step, b:] = corner[:, :b]
        blocks[j][rows + step :, :b] = corner[:, b:]
        blocks[j][rows + step :, b:] = corner[:, b:]


def sum_own_kernel(right, left, local, out):
    rows = right.shape[1]
    b = rows // 2
    step = (right.shape[0] - rows) // 2
    total = right[...].astype(F32) + left[...].astype(F32) + local[...].astype(F32)
    corner_hi, corner_lo = halves(total[rows : rows + step, b:] + total[rows + step :, :b])
    out[:rows, :] = total[:rows].astype(BF)
    out[rows : rows + step, :b] = total[rows : rows + step, :b].astype(BF)
    out[rows : rows + step, b:] = corner_hi
    out[rows + step :, :b] = corner_lo
    out[rows + step :, b:] = corner_lo


def middle_kernel(owners, inv, *refs):
    n = 8
    coupled = refs[:n]
    link, _, terms, maps, whole, corner, tail = refs[n:]
    me = lax.axis_index("narrow")
    rows = inv.shape[0]
    b = rows // 2
    step = b // n
    for j in range(n):
        g = lax.rem(me + j, n)
        block = coupled[j]
        whole[pl.ds(pl.multiple_of(g * rows, rows), rows), :] = block[:rows, :]
        at = pl.ds(pl.multiple_of(g * step, step), step)
        tail[at, :] = block[rows : rows + step, :b]
        corner[at, :] = block[rows : rows + step, b:].astype(F32) + block[
            rows + step :, :b
        ].astype(F32)
    applied = mm(inv[...], whole[...], NN)
    app = applied.astype(BF)
    first_hi, first_lo = halves(mm(tail[...], link[...], NN))
    maps[:b, :] = first_hi
    maps[b : 2 * b, :] = first_lo
    inner = mm2(corner[...], link[...], NN)
    maps[2 * b :, :] = mm2(inner, link[...], TN).astype(BF)
    for g in range(n):
        block = mm(inv[:, g * rows : (g + 1) * rows], app, TN).astype(BF)
        terms[owners[0, g], :rows, :] = block
    state_hi, state_lo = halves(jnp.where(owners[0, n - 1] == me, applied[rows - b :, :], 0.0).T)
    head_hi, head_lo = halves(mm(app, inv[:, :b], TN))
    cols = (terms.shape[1] - rows) // 2
    for j in range(n):
        at = slice(j * cols, (j + 1) * cols)
        terms[j, rows : rows + cols, :b] = state_hi[at]
        terms[j, rows : rows + cols, b:] = head_hi[at]
        terms[j, rows + cols :, :b] = state_lo[at]
        terms[j, rows + cols :, b:] = head_lo[at]


def sum_terms_kernel(parts, shared, link, *refs):
    kept, packed, spread = refs[-3:]
    rows = kept.shape[0]
    b = link.shape[0]
    cols = spread.shape[1]
    total = parts[0].astype(F32)
    for j in range(1, parts.shape[0]):
        total += parts[j].astype(F32)
    kept[...] = total[:rows]
    packed[:rows, :] = total[:rows].astype(BF)
    packed[rows:, :] = shared[...]
    ends = total[rows : rows + cols] + total[rows + cols :]
    head = mm2(ends[:, b:], link[...], NN)
    for j in range(spread.shape[0]):
        spread[j, :, :b] = ends[:, :b]
        spread[j, :, b:] = head


def stack_kernel(*refs):
    out = refs[-1]
    for j in range(out.shape[0]):
        out[j] = refs[j][...]


def times_map(value, hi, lo, dims):
    vh, vl = halves(value)
    return mm(vh, hi, dims) + (mm(vl, hi, dims) + mm(vh, lo, dims))


def chain_kernel(*refs):
    ags = refs[:2]
    mapss = refs[2:6], refs[6:10]
    link, out, ag, maps, states, incoming, sems = refs[10:]
    b = link.shape[0]
    length = states.shape[0]
    wide = lax.axis_index("wide")
    here = lax.rem(wide, 2)
    x = lax.rem(lax.div(wide, 2), 4)
    y = lax.div(wide, 8)
    copies = []
    for side, ag_part, map_parts in ((here, ags[0], mapss[0]), (1 - here, ags[1], mapss[1])):
        copies.append((ag_part, ag.at[side]))
        for j in range(4):
            for k in range(4):
                at = lax.rem(y + j, 4) * 4 + lax.rem(x + k, 4)
                copies.append((map_parts[j].at[k], maps.at[side, at]))
    copies = [pltpu.make_async_copy(p, q, sems.at[i]) for i, (p, q) in enumerate(copies)]
    for copy in copies:
        copy.start()
    for copy in copies:
        copy.wait()
    state = jnp.zeros((out.shape[1], b), F32)
    for w in range(length):
        states[w] = state
        if w + 1 < length:
            at = (w % 2, w // 2)
            moved = times_map(state, maps[(*at, slice(0, b))], maps[(*at, slice(b, 2 * b))], NT)
            state = ag[(*at, slice(None), slice(0, b))] - moved
    back = jnp.zeros_like(state)
    for w in range(length - 1, -1, -1):
        incoming[w] = back
        if w > 0:
            at = (w % 2, w // 2)
            vh, vl = halves(states[w])
            corner = maps[(*at, slice(2 * b, 3 * b))]
            local = ag[(*at, slice(None), slice(b, 2 * b))] - (mm(vh, corner, NN) + mm(vl, corner, NN))
            moved = times_map(back, maps[(*at, slice(0, b))], maps[(*at, slice(b, 2 * b))], NN)
            back = local - moved
    mine = mm2(states[wide], link[...], NT)
    last = incoming[wide]
    for j in range(out.shape[0]):
        out[j, :, :b] = mine
        out[j, :, b:] = last


def final_kernel(
    parent, owners, kept, gathered, z, cpl, inv, fl, leaf_out, sep_out, zs
):
    b = inv.shape[1]
    rows = kept.shape[0]
    zh, zl = halves(z[...])
    zs[0] = zh
    zs[1] = zl

    def fix(g, start, count):
        part = gathered[g, pl.ds(rows + start, count), :]
        return mm(part, zs[0], NT) + mm(part, zs[1], NT)

    sep_out[...] = kept[...] - fix(held_group(owners), 0, rows)
    for i in range(inv.shape[0]):
        acc = fl[i * b : (i + 1) * b, :].astype(F32)
        for k in range(cpl.shape[1]):
            p = parent[k, i]
            g = lax.div(p, 2)
            at = pl.multiple_of(lax.rem(p, 2) * b, b)
            block = gathered[owners[0, g], pl.ds(at, b), :].astype(F32)
            block = (block - fix(g, at, b)).astype(BF)
            acc -= mm(cpl[i, k], block, TN)
        leaf_out[i * b : (i + 1) * b, :] = mm(inv[i], acc.astype(BF), TN)


def swap(value, axis, by):
    n = lax.axis_size(axis)
    return lax.ppermute(value, axis, [(i, i ^ by) for i in range(n)])


def turned(value, by):
    n = lax.axis_size("narrow")
    return lax.ppermute(value, "narrow", [(i, (i + by) % n) for i in range(n)])


def ring_sum(blocks):
    def plus(value, block):
        return (value.astype(F32) + block.astype(F32)).astype(BF)

    right = turned(blocks[4], 1)
    left = turned(blocks[5], -1)
    right = turned(plus(right, blocks[3]), 1)
    left = turned(plus(left, blocks[6]), -1)
    right = turned(plus(right, blocks[2]), 1)
    left = turned(plus(left, blocks[7]), -1)
    right = turned(plus(right, blocks[1]), 1)
    return right, left


def ring_gather(block):
    ahead = [block]
    behind = [block]
    for _ in range(3):
        behind.append(turned(behind[-1], 1))
        ahead.append(turned(ahead[-1], -1))
    behind.append(turned(behind[-1], 1))
    return ahead + behind[:0:-1]


def turned_wide(value, along, by):
    def source(i):
        y, x, core = i // 8, (i // 2) % 4, i % 2
        y, x = (y, (x + by) % 4) if along == "x" else ((y + by) % 4, x)
        return (y * 4 + x) * 2 + core

    return lax.ppermute(value, "wide", [(source(i), i) for i in range(32)])


def per_device(
    leaf_rhs, leaf_inv, leaf_coupling, leaf_parent, sep_rhs, sep_inv, sep_link, row_owner
):
    b = leaf_inv.shape[1]
    leaf_count = leaf_inv.shape[0]
    sketch = leaf_rhs.shape[1]
    rows = sep_inv.shape[0]
    n = lax.axis_size("narrow")
    chain_len = lax.axis_size("wide")
    chips = chain_len // 2
    all_rows = sep_inv.shape[1]
    cols = sketch // n
    parent = leaf_parent.T
    shape = jax.ShapeDtypeStruct
    held = pltpu.VMEM

    extra = rows + 2 * (b // n)
    fl, shared, *blocks = call(
        leaf_forward_kernel,
        "leaf_forward",
        (shape((leaf_count * b, sketch), BF), shape((all_rows, 2 * b), BF))
        + (held((extra, sketch), BF),) * n,
        [SMEM] * 2 + [VMEM] * 5,
        [pltpu.VMEM((all_rows + 2 * b, sketch), F32)],
        flops=2 * 12 * b * b * sketch,
        moved=4 << 20,
    )(parent, row_owner, leaf_rhs, leaf_inv, leaf_coupling, sep_rhs, sep_inv)
    right, left = ring_sum(blocks)
    own = call(sum_own_kernel, "sum_own", held((extra, sketch), BF), [VMEM] * 3, moved=1 << 18)(
        right, left, blocks[0]
    )
    coupled = ring_gather(own)

    shared = lax.psum_scatter(shared, "narrow", scatter_dimension=0, tiled=True)
    terms, maps = call(
        middle_kernel,
        "middle",
        (shape((n, rows + 2 * cols, sketch), BF), shape((3 * b, b), BF)),
        [SMEM] + [VMEM] * (2 + n) + [ANY],
        [pltpu.VMEM((all_rows, sketch), BF), pltpu.VMEM((b, b), F32), pltpu.VMEM((b, b), BF)],
        flops=4 * rows * all_rows * sketch,
        moved=4 << 20,
    )(row_owner, sep_inv, *coupled, sep_link, shared)
    maps = call(stack_kernel, "stack_maps", shape((4, 3 * b, b), BF), [VMEM] * 4, moved=1 << 18)(
        maps, *[turned_wide(maps, "x", k) for k in (1, 2, 3)]
    )
    maps = [maps] + [turned_wide(maps, "y", k) for k in (1, 2, 3)]
    maps_other = [swap(part, "wide", 1) for part in maps]

    terms = lax.all_to_all(terms, "narrow", 0, 0, tiled=True)
    kept, packed, ag = call(
        sum_terms_kernel,
        "sum_terms",
        (
            shape((rows, sketch), F32),
            shape((2 * rows, sketch), BF),
            shape((chips, cols, 2 * b), F32),
        ),
        [VMEM] * 3 + [ANY] * 4,
        moved=2 << 20,
    )(terms, shared, sep_link, *maps_other)
    gathered = lax.all_gather(packed, "narrow", axis=0, tiled=False)

    same_core = [[2 * q + c for q in range(chips)] for c in range(2)]
    ag = lax.all_to_all(ag, "wide", 0, 0, tiled=True, axis_index_groups=same_core)
    ag_other = swap(ag, "wide", 1)
    z = call(
        chain_kernel,
        "chain",
        shape((n, cols, 2 * b), F32),
        [ANY] * 10 + [VMEM],
        [
            pltpu.VMEM((2, chips, cols, 2 * b), F32),
            pltpu.VMEM((2, chips, 3 * b, b), BF),
            pltpu.VMEM((chain_len, cols, b), F32),
            pltpu.VMEM((chain_len, cols, b), F32),
            pltpu.SemaphoreType.DMA((2 + 2 * chips,)),
        ],
        flops=2 * 9 * chain_len * cols * b * b,
        moved=8 << 20,
    )(ag, ag_other, *maps, *maps_other, sep_link)
    z = lax.all_to_all(z, "narrow", 0, 0, tiled=True).reshape(sketch, 2 * b)

    leaf_out, sep_out = call(
        final_kernel,
        "final",
        (shape((leaf_count * b, sketch), F32), shape((rows, sketch), F32)),
        [SMEM] * 2 + [VMEM] * 6,
        [pltpu.VMEM((2, sketch, 2 * b), BF)],
        flops=2 * 40 * b * b * sketch,
        moved=6 << 20,
    )(parent, row_owner, kept, gathered, z, leaf_coupling, leaf_inv, fl)
    return leaf_out, sep_out


def solution(mesh):
    both = ("wide", "narrow")
    placed = (
        P(both, None),
        P(both, None, None),
        P(both, None, None, None),
        P(both, None),
        P(both, None),
        P(both, None),
        P("wide", None),
        P("wide", None),
    )
    return jax.shard_map(
        per_device,
        mesh=mesh,
        in_specs=placed,
        out_specs=(P(both, None), P(both, None)),
        check_vma=False,
    )
```

```python
import jax
import jax.numpy as jnp
from jax import lax
from jax.experimental import pallas as pl
from jax.experimental.pallas import tpu as pltpu
from jax.sharding import PartitionSpec as P

BF = jnp.bfloat16
F32 = jnp.float32
VMEM = pl.BlockSpec(memory_space=pltpu.VMEM)
SMEM = pl.BlockSpec(memory_space=pltpu.SMEM)
ANY = pl.BlockSpec(memory_space=pl.ANY)
MIB = 1024 * 1024

NN = (((1,), (0,)), ((), ()))
NT = (((1,), (1,)), ((), ()))
TN = (((0,), (0,)), ((), ()))


def mm(a, b, dims):
    return lax.dot_general(a, b, dims, preferred_element_type=F32)


def halves(v):
    hi = v.astype(BF)
    return hi, (v - hi.astype(F32)).astype(BF)


def mm3(a, b, dims):
    ah, al = halves(a)
    bh, bl = halves(b)
    return mm(ah, bh, dims) + (mm(al, bh, dims) + mm(ah, bl, dims))


def mm2(a, b_exact, dims):
    ah = a.astype(BF)
    rest = a - ah.astype(F32)
    al = rest.astype(BF)
    ax = (rest - al.astype(F32)).astype(BF)
    return mm(ah, b_exact, dims) + (mm(al, b_exact, dims) + mm(ax, b_exact, dims))


def call(kernel, name, outs, ins, scratch=(), flops=0, moved=0, limit=20):
    return pl.pallas_call(
        kernel,
        name=name,
        out_shape=outs,
        in_specs=ins,
        out_specs=jax.tree.map(lambda _: VMEM, outs, is_leaf=lambda o: hasattr(o, "dtype")),
        scratch_shapes=list(scratch),
        compiler_params=pltpu.CompilerParams(vmem_limit_bytes=limit * MIB),
        cost_estimate=pl.CostEstimate(flops=flops, bytes_accessed=moved, transcendentals=0),
    )


def near(value):
    return pltpu.with_memory_space_constraint(value, pltpu.VMEM)


def held_group(owners):
    me = lax.axis_index("narrow")
    group = jnp.int32(0)
    for g in range(1, 8):
        group = jnp.where(owners[0, g] == me, g, group)
    return group


def leaf_forward_kernel(parent, owners, rhs, inv, cpl, sep_rhs, sep_inv, fl, shared, *refs):
    blocks = refs[:-1]
    acc = refs[-1]
    b = inv.shape[1]
    rows = sep_rhs.shape[0]
    n = len(blocks)
    me = lax.axis_index("narrow")
    acc[...] = jnp.zeros_like(acc)
    start = pl.multiple_of(held_group(owners) * rows, rows)
    acc[pl.ds(start, rows), :] = sep_rhs[...].astype(F32)
    for i in range(inv.shape[0]):
        f = mm(inv[i], rhs[i * b : (i + 1) * b, :], NN).astype(BF)
        fl[i * b : (i + 1) * b, :] = f
        for k in range(cpl.shape[1]):
            at = pl.ds(pl.multiple_of(parent[k, i] * b, b), b)
            acc[at, :] -= mm(cpl[i, k], f, NN)
    head = sep_inv[:, :b]
    corner_hi, corner_lo = halves(mm(head, head, TN))
    acc[n * rows : n * rows + b, :b] = corner_hi.astype(F32)
    acc[n * rows : n * rows + b, b:] = corner_lo.astype(F32)
    holds_last = owners[0, n - 1] == me
    acc[n * rows + b :, :b] = jnp.where(holds_last, head[rows - b :, :].astype(F32), 0.0)
    rows_at = lax.broadcasted_iota(jnp.int32, (rows, b), 0)
    cols_at = lax.broadcasted_iota(jnp.int32, (rows, b), 1)
    pick = jnp.where(holds_last & (rows_at == cols_at + (rows - b)), 1.0, 0.0).astype(BF)
    ends = jnp.concatenate([head, pick], axis=1)
    for g in range(n):
        at = slice(g * rows, (g + 1) * rows)
        shared[at, :] = mm(sep_inv[:, at], ends, TN).astype(BF)
    step = b // n
    for j in range(n):
        g = lax.rem(me + j, n)
        blocks[j][:rows, :] = acc[pl.ds(pl.multiple_of(g * rows, rows), rows), :].astype(BF)
        corner = acc[pl.ds(pl.multiple_of(n * rows + g * step, step), step), :].astype(BF)
        tail = acc[pl.ds(pl.multiple_of(n * rows + b + g * step, step), step), :b].astype(BF)
        blocks[j][rows : rows + step, :b] = tail
        blocks[j][rows : rows + step, b:] = corner[:, :b]
        blocks[j][rows + step :, :b] = corner[:, b:]
        blocks[j][rows + step :, b:] = corner[:, b:]


def sum_own_kernel(right, left, local, out):
    rows = right.shape[1]
    b = rows // 2
    step = (right.shape[0] - rows) // 2
    total = right[...].astype(F32) + left[...].astype(F32) + local[...].astype(F32)
    corner_hi, corner_lo = halves(total[rows : rows + step, b:] + total[rows + step :, :b])
    out[:rows, :] = total[:rows].astype(BF)
    out[rows : rows + step, :b] = total[rows : rows + step, :b].astype(BF)
    out[rows : rows + step, b:] = corner_hi
    out[rows + step :, :b] = corner_lo
    out[rows + step :, b:] = corner_lo


def middle_kernel(owners, inv, *refs):
    n = 8
    coupled = refs[:n]
    link, _, terms, maps, whole, corner, tail = refs[n:]
    me = lax.axis_index("narrow")
    rows = inv.shape[0]
    b = rows // 2
    step = b // n
    for j in range(n):
        g = lax.rem(me + j, n)
        block = coupled[j]
        whole[pl.ds(pl.multiple_of(g * rows, rows), rows), :] = block[:rows, :]
        at = pl.ds(pl.multiple_of(g * step, step), step)
        tail[at, :] = block[rows : rows + step, :b]
        corner[at, :] = block[rows : rows + step, b:].astype(F32) + block[
            rows + step :, :b
        ].astype(F32)
    applied = mm(inv[...], whole[...], NN)
    app = applied.astype(BF)
    first_hi, first_lo = halves(mm(tail[...], link[...], NN))
    maps[:b, :] = first_hi
    maps[b : 2 * b, :] = first_lo
    inner = mm2(corner[...], link[...], NN)
    maps[2 * b :, :] = mm2(inner, link[...], TN).astype(BF)
    for g in range(n):
        block = mm(inv[:, g * rows : (g + 1) * rows], app, TN).astype(BF)
        terms[owners[0, g], :rows, :] = block
    state_hi, state_lo = halves(jnp.where(owners[0, n - 1] == me, applied[rows - b :, :], 0.0).T)
    head_hi, head_lo = halves(mm(app, inv[:, :b], TN))
    cols = (terms.shape[1] - rows) // 2
    for j in range(n):
        at = slice(j * cols, (j + 1) * cols)
        terms[j, rows : rows + cols, :b] = state_hi[at]
        terms[j, rows : rows + cols, b:] = head_hi[at]
        terms[j, rows + cols :, :b] = state_lo[at]
        terms[j, rows + cols :, b:] = head_lo[at]


def sum_ends_kernel(parts, link, *refs):
    spread = refs[-1]
    b = link.shape[0]
    cols = spread.shape[1]
    rows = parts.shape[1] - 2 * cols
    total = parts[0, rows:, :].astype(F32)
    for j in range(1, parts.shape[0]):
        total += parts[j, rows:, :].astype(F32)
    ends = total[:cols] + total[cols:]
    head = mm2(ends[:, b:], link[...], NN)
    for j in range(spread.shape[0]):
        spread[j, :, :b] = ends[:, :b]
        spread[j, :, b:] = head


def sum_terms_kernel(parts, shared, _, kept, packed):
    rows = kept.shape[0]
    total = parts[0, :rows, :].astype(F32)
    for j in range(1, parts.shape[0]):
        total += parts[j, :rows, :].astype(F32)
    kept[...] = total
    packed[:rows, :] = total.astype(BF)
    packed[rows:, :] = shared[...]


def stack_kernel(*refs):
    out = refs[-1]
    for j in range(out.shape[0]):
        out[j] = refs[j][...]


def times_map(value, hi, lo, dims):
    vh, vl = halves(value)
    return mm(vh, hi, dims) + (mm(vl, hi, dims) + mm(vh, lo, dims))


def chain_kernel(*refs):
    ags = refs[:2]
    mapss = refs[2:6], refs[6:10]
    link, out, ag, maps, states, incoming, sems = refs[10:]
    b = link.shape[0]
    length = states.shape[0]
    wide = lax.axis_index("wide")
    here = lax.rem(wide, 2)
    x = lax.rem(lax.div(wide, 2), 4)
    y = lax.div(wide, 8)
    for side, ag_part, map_parts in ((here, ags[0], mapss[0]), (1 - here, ags[1], mapss[1])):
        for j in range(4):
            for k in range(4):
                at = lax.rem(y + j, 4) * 4 + lax.rem(x + k, 4)
                where = maps.at[side, at]
                pltpu.make_async_copy(map_parts[j].at[k], where, sems.at[side, at]).start()
        ag[side] = ag_part[...]
    state = jnp.zeros((out.shape[1], b), F32)
    for w in range(length):
        states[w] = state
        at = (w % 2, w // 2)
        pltpu.make_async_copy(mapss[0][0].at[0], maps.at[at], sems.at[at]).wait()
        if w + 1 < length:
            moved = times_map(state, maps[(*at, slice(0, b))], maps[(*at, slice(b, 2 * b))], NT)
            state = ag[(*at, slice(None), slice(0, b))] - moved
    back = jnp.zeros_like(state)
    for w in range(length - 1, -1, -1):
        incoming[w] = back
        if w > 0:
            at = (w % 2, w // 2)
            vh, vl = halves(states[w])
            corner = maps[(*at, slice(2 * b, 3 * b))]
            local = ag[(*at, slice(None), slice(b, 2 * b))] - (mm(vh, corner, NN) + mm(vl, corner, NN))
            moved = times_map(back, maps[(*at, slice(0, b))], maps[(*at, slice(b, 2 * b))], NN)
            back = local - moved
    mine = mm2(states[wide], link[...], NT).astype(BF)
    last = incoming[wide].astype(BF)
    for j in range(out.shape[0]):
        out[j, :, :b] = mine
        out[j, :, b:] = last


def before_kernel(parent, owners, gathered, cpl, fl, base, fix, own):
    b = cpl.shape[2]
    rows = own.shape[0]
    own[...] = gathered[held_group(owners), rows:, :]
    for i in range(cpl.shape[0]):
        at = slice(i * b, (i + 1) * b)
        value = fl[at, :].astype(F32)
        move = jnp.zeros((b, 2 * b), F32)
        for k in range(cpl.shape[1]):
            p = parent[k, i]
            g = lax.div(p, 2)
            start = pl.multiple_of(lax.rem(p, 2) * b, b)
            value -= mm(cpl[i, k], gathered[owners[0, g], pl.ds(start, b), :], TN)
            move += mm(cpl[i, k], gathered[g, pl.ds(rows + start, b), :], TN)
        base[at, :] = value
        fix[at, :] = move.astype(BF)


def final_kernel(kept, own, base, fix, z, inv, leaf_out, sep_out):
    b = inv.shape[1]
    sep_out[...] = kept[...] - mm(own[...], z[...], NT)
    for i in range(inv.shape[0]):
        at = slice(i * b, (i + 1) * b)
        middle = (base[at, :] + mm(fix[at, :], z[...], NT)).astype(BF)
        leaf_out[at, :] = mm(inv[i], middle, TN)


def swap(value, axis, by):
    n = lax.axis_size(axis)
    return lax.ppermute(value, axis, [(i, i ^ by) for i in range(n)])


def turned(value, by):
    n = lax.axis_size("narrow")
    return lax.ppermute(value, "narrow", [(i, (i + by) % n) for i in range(n)])


def ring_sum(blocks):
    def plus(value, block):
        return (value.astype(F32) + block.astype(F32)).astype(BF)

    right = turned(blocks[4], 1)
    left = turned(blocks[5], -1)
    right = turned(plus(right, blocks[3]), 1)
    left = turned(plus(left, blocks[6]), -1)
    right = turned(plus(right, blocks[2]), 1)
    left = turned(plus(left, blocks[7]), -1)
    right = turned(plus(right, blocks[1]), 1)
    return right, left


def ring_gather(block):
    ahead = [block]
    behind = [block]
    for _ in range(3):
        behind.append(turned(behind[-1], 1))
        ahead.append(turned(ahead[-1], -1))
    behind.append(turned(behind[-1], 1))
    return ahead + behind[:0:-1]


def turned_wide(value, along, by):
    def source(i):
        y, x, core = i // 8, (i // 2) % 4, i % 2
        y, x = (y, (x + by) % 4) if along == "x" else ((y + by) % 4, x)
        return (y * 4 + x) * 2 + core

    return lax.ppermute(value, "wide", [(source(i), i) for i in range(32)])


def per_device(
    leaf_rhs, leaf_inv, leaf_coupling, leaf_parent, sep_rhs, sep_inv, sep_link, row_owner
):
    b = leaf_inv.shape[1]
    leaf_count = leaf_inv.shape[0]
    sketch = leaf_rhs.shape[1]
    rows = sep_inv.shape[0]
    n = lax.axis_size("narrow")
    chain_len = lax.axis_size("wide")
    chips = chain_len // 2
    all_rows = sep_inv.shape[1]
    cols = sketch // n
    parent = leaf_parent.T
    shape = jax.ShapeDtypeStruct
    held = pltpu.VMEM

    extra = rows + 2 * (b // n)
    fl, shared, *blocks = call(
        leaf_forward_kernel,
        "leaf_forward",
        (shape((leaf_count * b, sketch), BF), shape((all_rows, 2 * b), BF))
        + (held((extra, sketch), BF),) * n,
        [SMEM] * 2 + [VMEM] * 5,
        [pltpu.VMEM((all_rows + 2 * b, sketch), F32)],
        flops=2 * 12 * b * b * sketch,
        moved=4 << 20,
        limit=56,
    )(parent, row_owner, leaf_rhs, leaf_inv, leaf_coupling, sep_rhs, sep_inv)
    right, left = ring_sum(blocks)
    own = call(sum_own_kernel, "sum_own", held((extra, sketch), BF), [VMEM] * 3, moved=1 << 18)(
        near(right), near(left), near(blocks[0])
    )
    coupled = [near(block) for block in ring_gather(own)]

    shared = lax.psum_scatter(shared, "narrow", scatter_dimension=0, tiled=True)
    terms, maps = call(
        middle_kernel,
        "middle",
        (held((n, rows + 2 * cols, sketch), BF), held((3 * b, b), BF)),
        [SMEM] + [VMEM] * (2 + n) + [ANY],
        [pltpu.VMEM((all_rows, sketch), BF), pltpu.VMEM((b, b), F32), pltpu.VMEM((b, b), BF)],
        flops=4 * rows * all_rows * sketch,
        moved=4 << 20,
        limit=56,
    )(row_owner, sep_inv, *coupled, sep_link, shared)
    maps = call(stack_kernel, "stack_maps", held((4, 3 * b, b), BF), [VMEM] * 4, moved=1 << 18)(
        near(maps), *[near(turned_wide(maps, "x", k)) for k in (1, 2, 3)]
    )
    maps = [maps] + [turned_wide(maps, "y", k) for k in (1, 2, 3)]
    maps_other = [swap(part, "wide", 1) for part in maps]

    terms = lax.all_to_all(terms, "narrow", 0, 0, tiled=True)
    terms = near(terms)
    ag = call(
        sum_ends_kernel,
        "sum_ends",
        held((chips, cols, 2 * b), F32),
        [VMEM] * 6,
        moved=1 << 19,
    )(terms, sep_link, *[near(part) for part in maps_other])
    kept, packed = call(
        sum_terms_kernel,
        "sum_terms",
        (pltpu.HBM((rows, sketch), F32), pltpu.HBM((2 * rows, sketch), BF)),
        [VMEM] * 2 + [ANY],
        moved=2 << 20,
    )(terms, shared, near(ag))
    gathered = lax.all_gather(packed, "narrow", axis=0, tiled=False)

    same_core = [[2 * q + c for q in range(chips)] for c in range(2)]
    ag = lax.all_to_all(ag, "wide", 0, 0, tiled=True, axis_index_groups=same_core)
    ag_other = near(swap(ag, "wide", 1))
    ag = near(ag)
    z = call(
        chain_kernel,
        "chain",
        held((n, cols, 2 * b), BF),
        [VMEM] * 2 + [ANY] * 8 + [VMEM],
        [
            pltpu.VMEM((2, chips, cols, 2 * b), F32),
            pltpu.VMEM((2, chips, 3 * b, b), BF),
            pltpu.VMEM((chain_len, cols, b), F32),
            pltpu.VMEM((chain_len, cols, b), F32),
            pltpu.SemaphoreType.DMA((2, chips)),
        ],
        flops=2 * 9 * chain_len * cols * b * b,
        moved=8 << 20,
        limit=56,
    )(ag, ag_other, *maps, *maps_other, sep_link)
    z = lax.all_to_all(z, "narrow", 0, 0, tiled=True).reshape(sketch, 2 * b)

    base, fix, own = call(
        before_kernel,
        "before",
        (
            held((leaf_count * b, sketch), F32),
            held((leaf_count * b, 2 * b), BF),
            held((rows, 2 * b), BF),
        ),
        [SMEM] * 2 + [VMEM] * 3,
        flops=2 * 16 * b * b * sketch,
        moved=4 << 20,
    )(parent, row_owner, gathered, leaf_coupling, fl)
    leaf_out, sep_out = call(
        final_kernel,
        "final",
        (shape((leaf_count * b, sketch), F32), shape((rows, sketch), F32)),
        [VMEM] * 6,
        flops=2 * 16 * b * b * sketch,
        moved=2 << 20,
    )(kept, near(own), near(base), near(fix), near(z), leaf_inv)
    return leaf_out, sep_out


def solution(mesh):
    both = ("wide", "narrow")
    placed = (
        P(both, None),
        P(both, None, None),
        P(both, None, None, None),
        P(both, None),
        P(both, None),
        P(both, None),
        P("wide", None),
        P("wide", None),
    )
    return jax.shard_map(
        per_device,
        mesh=mesh,
        in_specs=placed,
        out_specs=(P(both, None), P(both, None)),
        check_vma=False,
    )
```

```python
import jax
import jax.numpy as jnp
from jax import lax
from jax.experimental import pallas as pl
from jax.experimental.pallas import tpu as pltpu
from jax.sharding import PartitionSpec as P

BF = jnp.bfloat16
F32 = jnp.float32
VMEM = pl.BlockSpec(memory_space=pltpu.VMEM)
SMEM = pl.BlockSpec(memory_space=pltpu.SMEM)
ANY = pl.BlockSpec(memory_space=pl.ANY)
MIB = 1024 * 1024

NN = (((1,), (0,)), ((), ()))
NT = (((1,), (1,)), ((), ()))
TN = (((0,), (0,)), ((), ()))


def mm(a, b, dims):
    return lax.dot_general(a, b, dims, preferred_element_type=F32)


def halves(v):
    hi = v.astype(BF)
    return hi, (v - hi.astype(F32)).astype(BF)


def mm3(a, b, dims):
    ah, al = halves(a)
    bh, bl = halves(b)
    return mm(ah, bh, dims) + (mm(al, bh, dims) + mm(ah, bl, dims))


def mm2(a, b_exact, dims):
    ah = a.astype(BF)
    rest = a - ah.astype(F32)
    al = rest.astype(BF)
    ax = (rest - al.astype(F32)).astype(BF)
    return mm(ah, b_exact, dims) + (mm(al, b_exact, dims) + mm(ax, b_exact, dims))


def call(kernel, name, outs, ins, scratch=(), flops=0, moved=0, limit=20):
    return pl.pallas_call(
        kernel,
        name=name,
        out_shape=outs,
        in_specs=ins,
        out_specs=jax.tree.map(lambda _: VMEM, outs, is_leaf=lambda o: hasattr(o, "dtype")),
        scratch_shapes=list(scratch),
        compiler_params=pltpu.CompilerParams(vmem_limit_bytes=limit * MIB),
        cost_estimate=pl.CostEstimate(flops=flops, bytes_accessed=moved, transcendentals=0),
    )


def near(value):
    return pltpu.with_memory_space_constraint(value, pltpu.VMEM)


def held_group(owners):
    me = lax.axis_index("narrow")
    group = jnp.int32(0)
    for g in range(1, 8):
        group = jnp.where(owners[0, g] == me, g, group)
    return group


def leaf_forward_kernel(parent, owners, rhs, inv, cpl, sep_rhs, sep_inv, fl, shared, *refs):
    blocks = refs[:-1]
    acc = refs[-1]
    b = inv.shape[1]
    rows = sep_rhs.shape[0]
    n = len(blocks)
    me = lax.axis_index("narrow")
    acc[...] = jnp.zeros_like(acc)
    start = pl.multiple_of(held_group(owners) * rows, rows)
    acc[pl.ds(start, rows), :] = sep_rhs[...].astype(F32)
    for i in range(inv.shape[0]):
        f = mm(inv[i], rhs[i * b : (i + 1) * b, :], NN).astype(BF)
        fl[i * b : (i + 1) * b, :] = f
        for k in range(cpl.shape[1]):
            at = pl.ds(pl.multiple_of(parent[k, i] * b, b), b)
            acc[at, :] -= mm(cpl[i, k], f, NN)
    head = sep_inv[:, :b]
    corner_hi, corner_lo = halves(mm(head, head, TN))
    acc[n * rows : n * rows + b, :b] = corner_hi.astype(F32)
    acc[n * rows : n * rows + b, b:] = corner_lo.astype(F32)
    holds_last = owners[0, n - 1] == me
    acc[n * rows + b :, :b] = jnp.where(holds_last, head[rows - b :, :].astype(F32), 0.0)
    rows_at = lax.broadcasted_iota(jnp.int32, (rows, b), 0)
    cols_at = lax.broadcasted_iota(jnp.int32, (rows, b), 1)
    pick = jnp.where(holds_last & (rows_at == cols_at + (rows - b)), 1.0, 0.0).astype(BF)
    ends = jnp.concatenate([head, pick], axis=1)
    for g in range(n):
        at = slice(g * rows, (g + 1) * rows)
        shared[at, :] = mm(sep_inv[:, at], ends, TN).astype(BF)
    step = b // n
    for j in range(n):
        g = lax.rem(me + j, n)
        blocks[j][:rows, :] = acc[pl.ds(pl.multiple_of(g * rows, rows), rows), :].astype(BF)
        corner = acc[pl.ds(pl.multiple_of(n * rows + g * step, step), step), :].astype(BF)
        tail = acc[pl.ds(pl.multiple_of(n * rows + b + g * step, step), step), :b].astype(BF)
        blocks[j][rows : rows + step, :b] = tail
        blocks[j][rows : rows + step, b:] = corner[:, :b]
        blocks[j][rows + step :, :b] = corner[:, b:]
        blocks[j][rows + step :, b:] = corner[:, b:]


def sum_own_kernel(right, left, local, out):
    rows = right.shape[1]
    b = rows // 2
    step = (right.shape[0] - rows) // 2
    total = right[...].astype(F32) + left[...].astype(F32) + local[...].astype(F32)
    corner_hi, corner_lo = halves(total[rows : rows + step, b:] + total[rows + step :, :b])
    out[:rows, :] = total[:rows].astype(BF)
    out[rows : rows + step, :b] = total[rows : rows + step, :b].astype(BF)
    out[rows : rows + step, b:] = corner_hi
    out[rows + step :, :b] = corner_lo
    out[rows + step :, b:] = corner_lo


def middle_kernel(owners, inv, *refs):
    n = 8
    coupled = refs[:n]
    link, _, terms, maps, whole, corner, tail = refs[n:]
    me = lax.axis_index("narrow")
    rows = inv.shape[0]
    b = rows // 2
    step = b // n
    for j in range(n):
        g = lax.rem(me + j, n)
        block = coupled[j]
        whole[pl.ds(pl.multiple_of(g * rows, rows), rows), :] = block[:rows, :]
        at = pl.ds(pl.multiple_of(g * step, step), step)
        tail[at, :] = block[rows : rows + step, :b]
        corner[at, :] = block[rows : rows + step, b:].astype(F32) + block[
            rows + step :, :b
        ].astype(F32)
    first_hi, first_lo = halves(mm(tail[...], link[...], NN))
    maps[:b, :] = first_hi
    maps[b : 2 * b, :] = first_lo
    inner = mm2(corner[...], link[...], NN)
    maps[2 * b :, :] = mm2(inner, link[...], TN).astype(BF)
    applied = mm(inv[...], whole[...], NN)
    app = applied.astype(BF)
    for g in range(n):
        block = mm(inv[:, g * rows : (g + 1) * rows], app, TN).astype(BF)
        terms[owners[0, g], :rows, :] = block
    state_hi, state_lo = halves(jnp.where(owners[0, n - 1] == me, applied[rows - b :, :], 0.0).T)
    head = mm2(mm(app, inv[:, :b], TN), link[...], NN).astype(BF)
    half = terms.shape[1] - rows
    half = half // 3
    for j in range(n):
        at = 2 * half * j
        terms[j, rows : rows + 2 * half, :b] = state_hi[at : at + 2 * half]
        terms[j, rows : rows + 2 * half, b:] = head[at : at + 2 * half]
        terms[j, rows + 2 * half :, :b] = state_lo[at : at + half]
        terms[j, rows + 2 * half :, b:] = state_lo[at + half : at + 2 * half]


def sum_ends_kernel(parts, spread):
    b = spread.shape[2] // 2
    rows = parts.shape[1] - spread.shape[1]
    half = spread.shape[1] // 3
    cols = 2 * half
    total = parts[0, rows:, :].astype(F32)
    for j in range(1, parts.shape[0]):
        total += parts[j, rows:, :].astype(F32)
    low = jnp.concatenate([total[cols:, :b], total[cols:, b:]], axis=0)
    state_hi, state_lo = halves(total[:cols, :b] + low)
    head = total[:cols, b:].astype(BF)
    for j in range(spread.shape[0]):
        spread[j, :cols, :b] = state_hi
        spread[j, :cols, b:] = head
        spread[j, cols:, :b] = state_lo[:half]
        spread[j, cols:, b:] = state_lo[half:]


def sum_terms_kernel(parts, shared, *refs):
    kept, packed = refs[-2:]
    rows = kept.shape[0]
    total = parts[0, :rows, :].astype(F32)
    for j in range(1, parts.shape[0]):
        total += parts[j, :rows, :].astype(F32)
    kept[...] = total
    packed[:rows, :] = total.astype(BF)
    packed[rows:, :] = shared[...]


def stack_kernel(*refs):
    out = refs[-1]
    for j in range(out.shape[0]):
        out[j] = refs[j][...]


def times_map(value, both, dims):
    b = both.shape[1]
    vh, vl = halves(value)
    if dims is NN:
        wide = mm(vh, jnp.concatenate([both[:b], both[b:]], axis=1), NN)
    else:
        wide = mm(vh, both, NT)
    return (wide[:, :b] + wide[:, b:]) + mm(vl, both[:b], dims)


def chain_kernel(*refs):
    ags = refs[:2]
    mapss = refs[2:6], refs[6:10]
    link, out, ag, maps, states, incoming, sems = refs[10:]
    b = link.shape[0]
    length = states.shape[0]
    wide = lax.axis_index("wide")
    here = lax.rem(wide, 2)
    x = lax.rem(lax.div(wide, 2), 4)
    y = lax.div(wide, 8)
    for side, ag_part, map_parts in ((here, ags[0], mapss[0]), (1 - here, ags[1], mapss[1])):
        for j in range(4):
            for k in range(4):
                at = lax.rem(y + j, 4) * 4 + lax.rem(x + k, 4)
                where = maps.at[side, at]
                pltpu.make_async_copy(map_parts[j].at[k], where, sems.at[side, at]).start()
        cols = out.shape[1]
        for q in range(ag_part.shape[0]):
            low = ag_part[q, cols:, :].astype(F32)
            low = jnp.concatenate([low[:, :b], low[:, b:]], axis=0)
            ag[side, q, :, :b] = ag_part[q, :cols, :b].astype(F32) + low
            ag[side, q, :, b:] = ag_part[q, :cols, b:].astype(F32)
    state = jnp.zeros((out.shape[1], b), F32)
    for w in range(length):
        states[w] = state
        at = (w % 2, w // 2)
        pltpu.make_async_copy(mapss[0][0].at[0], maps.at[at], sems.at[at]).wait()
        if w + 1 < length:
            moved = times_map(state, maps[(*at, slice(0, 2 * b))], NT)
            state = ag[(*at, slice(None), slice(0, b))] - moved
    back = jnp.zeros_like(state)
    for w in range(length - 1, -1, -1):
        incoming[w] = back
        if w > 0:
            at = (w % 2, w // 2)
            pair = jnp.concatenate(halves(states[w]), axis=1)
            corner = maps[(*at, slice(2 * b, 3 * b))]
            corner = mm(pair, jnp.concatenate([corner, corner], axis=0), NN)
            local = ag[(*at, slice(None), slice(b, 2 * b))] - corner
            moved = times_map(back, maps[(*at, slice(0, 2 * b))], NN)
            back = local - moved
    mine = mm2(states[wide], link[...], NT).astype(BF)
    last = incoming[wide].astype(BF)
    for j in range(out.shape[0]):
        out[j, :, :b] = mine
        out[j, :, b:] = last


def before_kernel(parent, owners, gathered, cpl, fl, base, fix, own):
    b = cpl.shape[2]
    rows = own.shape[0]
    own[...] = gathered[held_group(owners), rows:, :]
    for i in range(cpl.shape[0]):
        at = slice(i * b, (i + 1) * b)
        value = fl[at, :].astype(F32)
        move = jnp.zeros((b, 2 * b), F32)
        for k in range(cpl.shape[1]):
            p = parent[k, i]
            g = lax.div(p, 2)
            start = pl.multiple_of(lax.rem(p, 2) * b, b)
            value -= mm(cpl[i, k], gathered[owners[0, g], pl.ds(start, b), :], TN)
            move += mm(cpl[i, k], gathered[g, pl.ds(rows + start, b), :], TN)
        base[at, :] = value
        fix[at, :] = move.astype(BF)


def final_kernel(kept, own, base, fix, z, inv, leaf_out, sep_out):
    b = inv.shape[1]
    sep_out[...] = kept[...] - mm(own[...], z[...], NT)
    for i in range(inv.shape[0]):
        at = slice(i * b, (i + 1) * b)
        middle = (base[at, :] + mm(fix[at, :], z[...], NT)).astype(BF)
        leaf_out[at, :] = mm(inv[i], middle, TN)


def swap(value, axis, by):
    n = lax.axis_size(axis)
    return lax.ppermute(value, axis, [(i, i ^ by) for i in range(n)])


def turned(value, by):
    n = lax.axis_size("narrow")
    return lax.ppermute(value, "narrow", [(i, (i + by) % n) for i in range(n)])


def ring_sum(blocks):
    def plus(value, block):
        return (value.astype(F32) + block.astype(F32)).astype(BF)

    right = turned(blocks[4], 1)
    left = turned(blocks[5], -1)
    right = turned(plus(right, blocks[3]), 1)
    left = turned(plus(left, blocks[6]), -1)
    right = turned(plus(right, blocks[2]), 1)
    left = turned(plus(left, blocks[7]), -1)
    right = turned(plus(right, blocks[1]), 1)
    return right, left


def ring_gather(block):
    ahead = [block]
    behind = [block]
    for _ in range(3):
        behind.append(turned(behind[-1], 1))
        ahead.append(turned(ahead[-1], -1))
    behind.append(turned(behind[-1], 1))
    return ahead + behind[:0:-1]


def turned_wide(value, along, by):
    def source(i):
        y, x, core = i // 8, (i // 2) % 4, i % 2
        y, x = (y, (x + by) % 4) if along == "x" else ((y + by) % 4, x)
        return (y * 4 + x) * 2 + core

    return lax.ppermute(value, "wide", [(source(i), i) for i in range(32)])


def per_device(
    leaf_rhs, leaf_inv, leaf_coupling, leaf_parent, sep_rhs, sep_inv, sep_link, row_owner
):
    b = leaf_inv.shape[1]
    leaf_count = leaf_inv.shape[0]
    sketch = leaf_rhs.shape[1]
    rows = sep_inv.shape[0]
    n = lax.axis_size("narrow")
    chain_len = lax.axis_size("wide")
    chips = chain_len // 2
    all_rows = sep_inv.shape[1]
    cols = sketch // n
    parent = leaf_parent.T
    shape = jax.ShapeDtypeStruct
    held = pltpu.VMEM

    extra = rows + 2 * (b // n)
    fl, shared, *blocks = call(
        leaf_forward_kernel,
        "leaf_forward",
        (shape((leaf_count * b, sketch), BF), shape((all_rows, 2 * b), BF))
        + (held((extra, sketch), BF),) * n,
        [SMEM] * 2 + [VMEM] * 5,
        [pltpu.VMEM((all_rows + 2 * b, sketch), F32)],
        flops=2 * 12 * b * b * sketch,
        moved=4 << 20,
        limit=56,
    )(parent, row_owner, leaf_rhs, leaf_inv, leaf_coupling, sep_rhs, sep_inv)
    right, left = ring_sum(blocks)
    own = call(sum_own_kernel, "sum_own", held((extra, sketch), BF), [VMEM] * 3, moved=1 << 18)(
        near(right), near(left), near(blocks[0])
    )
    coupled = [near(block) for block in ring_gather(own)]

    shared = lax.psum_scatter(shared, "narrow", scatter_dimension=0, tiled=True)
    terms, maps = call(
        middle_kernel,
        "middle",
        (held((n, rows + cols + cols // 2, sketch), BF), held((3 * b, b), BF)),
        [SMEM] + [VMEM] * (2 + n) + [ANY],
        [pltpu.VMEM((all_rows, sketch), BF), pltpu.VMEM((b, b), F32), pltpu.VMEM((b, b), BF)],
        flops=4 * rows * all_rows * sketch,
        moved=4 << 20,
        limit=56,
    )(row_owner, sep_inv, *coupled, sep_link, shared)
    maps = call(stack_kernel, "stack_maps", held((4, 3 * b, b), BF), [VMEM] * 4, moved=1 << 18)(
        near(maps), *[near(turned_wide(maps, "x", k)) for k in (1, 2, 3)]
    )
    maps = [maps] + [turned_wide(maps, "y", k) for k in (1, 2, 3)]
    maps_other = [swap(part, "wide", 1) for part in maps]

    terms = lax.all_to_all(terms, "narrow", 0, 0, tiled=True)
    terms = near(terms)
    ag = call(
        sum_ends_kernel,
        "sum_ends",
        held((chips, cols + cols // 2, 2 * b), BF),
        [VMEM],
        moved=1 << 19,
    )(terms)
    kept, packed = call(
        sum_terms_kernel,
        "sum_terms",
        (pltpu.HBM((rows, sketch), F32), pltpu.HBM((2 * rows, sketch), BF)),
        [VMEM] * 7,
        moved=2 << 20,
    )(terms, shared, near(ag), *[near(part) for part in maps_other[:3]], near(maps[3]))
    gathered = lax.all_gather(packed, "narrow", axis=0, tiled=False)

    same_core = [[2 * q + c for q in range(chips)] for c in range(2)]
    ag = lax.all_to_all(ag, "wide", 0, 0, tiled=True, axis_index_groups=same_core)
    ag_other = near(swap(ag, "wide", 1))
    ag = near(ag)
    z = call(
        chain_kernel,
        "chain",
        held((n, cols, 2 * b), BF),
        [VMEM] * 2 + [ANY] * 7 + [VMEM] * 2,
        [
            pltpu.VMEM((2, chips, cols, 2 * b), F32),
            pltpu.VMEM((2, chips, 3 * b, b), BF),
            pltpu.VMEM((chain_len, cols, b), F32),
            pltpu.VMEM((chain_len, cols, b), F32),
            pltpu.SemaphoreType.DMA((2, chips)),
        ],
        flops=2 * 9 * chain_len * cols * b * b,
        moved=8 << 20,
        limit=56,
    )(ag, ag_other, *maps, *maps_other[:3], near(maps_other[3]), sep_link)
    z = lax.all_to_all(z, "narrow", 0, 0, tiled=True).reshape(sketch, 2 * b)

    base, fix, own = call(
        before_kernel,
        "before",
        (
            held((leaf_count * b, sketch), F32),
            held((leaf_count * b, 2 * b), BF),
            held((rows, 2 * b), BF),
        ),
        [SMEM] * 2 + [VMEM] * 3,
        flops=2 * 16 * b * b * sketch,
        moved=4 << 20,
    )(parent, row_owner, gathered, leaf_coupling, fl)
    leaf_out, sep_out = call(
        final_kernel,
        "final",
        (shape((leaf_count * b, sketch), F32), shape((rows, sketch), F32)),
        [VMEM] * 6,
        flops=2 * 16 * b * b * sketch,
        moved=2 << 20,
    )(kept, near(own), near(base), near(fix), near(z), leaf_inv)
    return leaf_out, sep_out


def solution(mesh):
    both = ("wide", "narrow")
    placed = (
        P(both, None),
        P(both, None, None),
        P(both, None, None, None),
        P(both, None),
        P(both, None),
        P(both, None),
        P("wide", None),
        P("wide", None),
    )
    return jax.shard_map(
        per_device,
        mesh=mesh,
        in_specs=placed,
        out_specs=(P(both, None), P(both, None)),
        check_vma=False,
    )
```

```python
import jax
import jax.numpy as jnp
from jax import lax
from jax.experimental import pallas as pl
from jax.experimental.pallas import tpu as pltpu
from jax.sharding import PartitionSpec as P

BF = jnp.bfloat16
F32 = jnp.float32
VMEM = pl.BlockSpec(memory_space=pltpu.VMEM)
SMEM = pl.BlockSpec(memory_space=pltpu.SMEM)
ANY = pl.BlockSpec(memory_space=pl.ANY)
MIB = 1024 * 1024

NN = (((1,), (0,)), ((), ()))
NT = (((1,), (1,)), ((), ()))
TN = (((0,), (0,)), ((), ()))


def mm(a, b, dims):
    return lax.dot_general(a, b, dims, preferred_element_type=F32)


def halves(v):
    hi = v.astype(BF)
    return hi, (v - hi.astype(F32)).astype(BF)


def mm3(a, b, dims):
    ah, al = halves(a)
    bh, bl = halves(b)
    return mm(ah, bh, dims) + (mm(al, bh, dims) + mm(ah, bl, dims))


def mm2(a, b_exact, dims):
    ah = a.astype(BF)
    rest = a - ah.astype(F32)
    al = rest.astype(BF)
    ax = (rest - al.astype(F32)).astype(BF)
    return mm(ah, b_exact, dims) + (mm(al, b_exact, dims) + mm(ax, b_exact, dims))


def call(kernel, name, outs, ins, scratch=(), flops=0, moved=0, limit=20):
    return pl.pallas_call(
        kernel,
        name=name,
        out_shape=outs,
        in_specs=ins,
        out_specs=jax.tree.map(lambda _: VMEM, outs, is_leaf=lambda o: hasattr(o, "dtype")),
        scratch_shapes=list(scratch),
        compiler_params=pltpu.CompilerParams(vmem_limit_bytes=limit * MIB),
        cost_estimate=pl.CostEstimate(flops=flops, bytes_accessed=moved, transcendentals=0),
    )


def near(value):
    return pltpu.with_memory_space_constraint(value, pltpu.VMEM)


def held_group(owners):
    me = lax.axis_index("narrow")
    group = jnp.int32(0)
    for g in range(1, 8):
        group = jnp.where(owners[0, g] == me, g, group)
    return group


def leaf_forward_kernel(parent, owners, rhs, inv, cpl, sep_rhs, sep_inv, fl, shared, *refs):
    blocks = refs[:-1]
    acc = refs[-1]
    b = inv.shape[1]
    rows = sep_rhs.shape[0]
    n = len(blocks)
    me = lax.axis_index("narrow")
    acc[...] = jnp.zeros_like(acc)
    start = pl.multiple_of(held_group(owners) * rows, rows)
    acc[pl.ds(start, rows), :] = sep_rhs[...].astype(F32)
    for i in range(inv.shape[0]):
        f = mm(inv[i], rhs[i * b : (i + 1) * b, :], NN).astype(BF)
        fl[i * b : (i + 1) * b, :] = f
        for k in range(cpl.shape[1]):
            at = pl.ds(pl.multiple_of(parent[k, i] * b, b), b)
            acc[at, :] -= mm(cpl[i, k], f, NN)
    head = sep_inv[:, :b]
    corner_hi, corner_lo = halves(mm(head, head, TN))
    acc[n * rows : n * rows + b, :b] = corner_hi.astype(F32)
    acc[n * rows : n * rows + b, b:] = corner_lo.astype(F32)
    holds_last = owners[0, n - 1] == me
    acc[n * rows + b :, :b] = jnp.where(holds_last, head[rows - b :, :].astype(F32), 0.0)
    rows_at = lax.broadcasted_iota(jnp.int32, (rows, b), 0)
    cols_at = lax.broadcasted_iota(jnp.int32, (rows, b), 1)
    pick = jnp.where(holds_last & (rows_at == cols_at + (rows - b)), 1.0, 0.0).astype(BF)
    ends = jnp.concatenate([head, pick], axis=1)
    for g in range(n):
        at = slice(g * rows, (g + 1) * rows)
        shared[at, :] = mm(sep_inv[:, at], ends, TN).astype(BF)
    step = b // n
    for j in range(n):
        g = lax.rem(me + j, n)
        blocks[j][:rows, :] = acc[pl.ds(pl.multiple_of(g * rows, rows), rows), :].astype(BF)
        corner = acc[pl.ds(pl.multiple_of(n * rows + g * step, step), step), :].astype(BF)
        tail = acc[pl.ds(pl.multiple_of(n * rows + b + g * step, step), step), :b].astype(BF)
        blocks[j][rows : rows + step, :b] = tail
        blocks[j][rows : rows + step, b:] = corner[:, :b]
        blocks[j][rows + step :, :b] = corner[:, b:]
        blocks[j][rows + step :, b:] = corner[:, b:]


def sum_own_kernel(right, left, local, out):
    rows = right.shape[1]
    b = rows // 2
    step = (right.shape[0] - rows) // 2
    total = right[...].astype(F32) + left[...].astype(F32) + local[...].astype(F32)
    corner_hi, corner_lo = halves(total[rows : rows + step, b:] + total[rows + step :, :b])
    out[:rows, :] = total[:rows].astype(BF)
    out[rows : rows + step, :b] = total[rows : rows + step, :b].astype(BF)
    out[rows : rows + step, b:] = corner_hi
    out[rows + step :, :b] = corner_lo
    out[rows + step :, b:] = corner_lo


def middle_kernel(owners, inv, *refs):
    n = 8
    coupled = refs[:n]
    link, _, terms, maps, whole, corner, tail = refs[n:]
    me = lax.axis_index("narrow")
    rows = inv.shape[0]
    b = rows // 2
    step = b // n
    for j in range(n):
        g = lax.rem(me + j, n)
        block = coupled[j]
        whole[pl.ds(pl.multiple_of(g * rows, rows), rows), :] = block[:rows, :]
        at = pl.ds(pl.multiple_of(g * step, step), step)
        tail[at, :] = block[rows : rows + step, :b]
        corner[at, :] = block[rows : rows + step, b:].astype(F32) + block[
            rows + step :, :b
        ].astype(F32)
    first_hi, first_lo = halves(mm(tail[...], link[...], NN))
    maps[:b, :] = first_hi
    maps[b : 2 * b, :] = first_lo
    inner = mm2(corner[...], link[...], NN)
    maps[2 * b :, :] = mm2(inner, link[...], TN).astype(BF)
    applied = mm(inv[...], whole[...], NN)
    app = applied.astype(BF)
    for g in range(n):
        block = mm(inv[:, g * rows : (g + 1) * rows], app, TN).astype(BF)
        terms[owners[0, g], :rows, :] = block
    state_hi, state_lo = halves(jnp.where(owners[0, n - 1] == me, applied[rows - b :, :], 0.0).T)
    head = mm2(mm(app, inv[:, :b], TN), link[...], NN).astype(BF)
    half = terms.shape[1] - rows
    half = half // 3
    for j in range(n):
        at = 2 * half * j
        terms[j, rows : rows + 2 * half, :b] = state_hi[at : at + 2 * half]
        terms[j, rows : rows + 2 * half, b:] = head[at : at + 2 * half]
        terms[j, rows + 2 * half :, :b] = state_lo[at : at + half]
        terms[j, rows + 2 * half :, b:] = state_lo[at + half : at + 2 * half]


def sum_ends_kernel(parts, spread):
    b = spread.shape[2] // 2
    rows = parts.shape[1] - spread.shape[1]
    half = spread.shape[1] // 3
    cols = 2 * half
    total = parts[0, rows:, :].astype(F32)
    for j in range(1, parts.shape[0]):
        total += parts[j, rows:, :].astype(F32)
    low = jnp.concatenate([total[cols:, :b], total[cols:, b:]], axis=0)
    state_hi, state_lo = halves(total[:cols, :b] + low)
    head = total[:cols, b:].astype(BF)
    for j in range(spread.shape[0]):
        spread[j, :cols, :b] = state_hi
        spread[j, :cols, b:] = head
        spread[j, cols:, :b] = state_lo[:half]
        spread[j, cols:, b:] = state_lo[half:]


def sum_terms_kernel(parts, shared, *refs):
    kept, packed = refs[-2:]
    rows = kept.shape[0]
    total = parts[0, :rows, :].astype(F32)
    for j in range(1, parts.shape[0]):
        total += parts[j, :rows, :].astype(F32)
    kept[...] = total
    packed[:rows, :] = total.astype(BF)
    packed[rows:, :] = shared[...]


def stack_kernel(*refs):
    out = refs[-1]
    for j in range(out.shape[0]):
        out[j] = refs[j][...]


def times_map(value, both, dims):
    b = both.shape[1]
    vh, vl = halves(value)
    if dims is NN:
        wide = mm(vh, jnp.concatenate([both[:b], both[b:]], axis=1), NN)
    else:
        wide = mm(vh, both, NT)
    return (wide[:, :b] + wide[:, b:]) + mm(vl, both[:b], dims)


def chain_kernel(*refs):
    ags = refs[:2]
    mapss = refs[2:6], refs[6:10]
    link, out, ag, maps, states, incoming, sems = refs[10:]
    b = link.shape[0]
    length = states.shape[0]
    wide = lax.axis_index("wide")
    here = lax.rem(wide, 2)
    x = lax.rem(lax.div(wide, 2), 4)
    y = lax.div(wide, 8)
    for side, ag_part, map_parts in ((here, ags[0], mapss[0]), (1 - here, ags[1], mapss[1])):
        for j in range(4):
            for k in range(4):
                at = lax.rem(y + j, 4) * 4 + lax.rem(x + k, 4)
                where = maps.at[side, at]
                pltpu.make_async_copy(map_parts[j].at[k], where, sems.at[side, at]).start()
        cols = out.shape[1]
        for q in range(ag_part.shape[0]):
            low = ag_part[q, cols:, :].astype(F32)
            low = jnp.concatenate([low[:, :b], low[:, b:]], axis=0)
            ag[side, q, :, :b] = ag_part[q, :cols, :b].astype(F32) + low
            ag[side, q, :, b:] = ag_part[q, :cols, b:].astype(F32)
    state = jnp.zeros((out.shape[1], b), F32)
    for w in range(length):
        states[w] = state
        at = (w % 2, w // 2)
        pltpu.make_async_copy(mapss[0][0].at[0], maps.at[at], sems.at[at]).wait()
        if w + 1 < length:
            moved = times_map(state, maps[(*at, slice(0, 2 * b))], NT)
            state = ag[(*at, slice(None), slice(0, b))] - moved
    back = jnp.zeros_like(state)
    for w in range(length - 1, -1, -1):
        incoming[w] = back
        if w > 0:
            at = (w % 2, w // 2)
            pair = jnp.concatenate(halves(states[w]), axis=1)
            corner = maps[(*at, slice(2 * b, 3 * b))]
            corner = mm(pair, jnp.concatenate([corner, corner], axis=0), NN)
            local = ag[(*at, slice(None), slice(b, 2 * b))] - corner
            moved = times_map(back, maps[(*at, slice(0, 2 * b))], NN)
            back = local - moved
    mine = mm2(states[wide], link[...], NT).astype(BF)
    last = incoming[wide].astype(BF)
    for j in range(out.shape[0]):
        out[j, :, :b] = mine
        out[j, :, b:] = last


def before_kernel(parent, owners, gathered, cpl, fl, base, fix, own):
    b = cpl.shape[2]
    rows = own.shape[0]
    own[...] = gathered[held_group(owners), rows:, :]
    for i in range(cpl.shape[0]):
        at = slice(i * b, (i + 1) * b)
        value = fl[at, :].astype(F32)
        move = jnp.zeros((b, 2 * b), F32)
        for k in range(cpl.shape[1]):
            p = parent[k, i]
            g = lax.div(p, 2)
            start = pl.multiple_of(lax.rem(p, 2) * b, b)
            value -= mm(cpl[i, k], gathered[owners[0, g], pl.ds(start, b), :], TN)
            move += mm(cpl[i, k], gathered[g, pl.ds(rows + start, b), :], TN)
        base[at, :] = value
        fix[at, :] = move.astype(BF)


def final_kernel(kept, own, base, fix, z, inv, leaf_out, sep_out):
    b = inv.shape[1]
    sep_out[...] = kept[...] - mm(own[...], z[...], NT)
    for i in range(inv.shape[0]):
        at = slice(i * b, (i + 1) * b)
        middle = (base[at, :] + mm(fix[at, :], z[...], NT)).astype(BF)
        leaf_out[at, :] = mm(inv[i], middle, TN)


def swap(value, axis, by):
    n = lax.axis_size(axis)
    return lax.ppermute(value, axis, [(i, i ^ by) for i in range(n)])


def turned(value, by):
    n = lax.axis_size("narrow")
    return lax.ppermute(value, "narrow", [(i, (i + by) % n) for i in range(n)])


def ring_sum(blocks):
    def plus(value, block):
        return (value.astype(F32) + block.astype(F32)).astype(BF)

    right = turned(blocks[4], 1)
    left = turned(blocks[5], -1)
    right = turned(plus(right, blocks[3]), 1)
    left = turned(plus(left, blocks[6]), -1)
    right = turned(plus(right, blocks[2]), 1)
    left = turned(plus(left, blocks[7]), -1)
    right = turned(plus(right, blocks[1]), 1)
    return right, left


def ring_gather(block):
    ahead = [block]
    behind = [block]
    for _ in range(3):
        behind.append(turned(behind[-1], 1))
        ahead.append(turned(ahead[-1], -1))
    behind.append(turned(behind[-1], 1))
    return ahead + behind[:0:-1]


def turned_wide(value, along, by):
    def source(i):
        y, x, core = i // 8, (i // 2) % 4, i % 2
        y, x = (y, (x + by) % 4) if along == "x" else ((y + by) % 4, x)
        return (y * 4 + x) * 2 + core

    return lax.ppermute(value, "wide", [(source(i), i) for i in range(32)])


def per_device(
    leaf_rhs, leaf_inv, leaf_coupling, leaf_parent, sep_rhs, sep_inv, sep_link, row_owner
):
    b = leaf_inv.shape[1]
    leaf_count = leaf_inv.shape[0]
    sketch = leaf_rhs.shape[1]
    rows = sep_inv.shape[0]
    n = lax.axis_size("narrow")
    chain_len = lax.axis_size("wide")
    chips = chain_len // 2
    all_rows = sep_inv.shape[1]
    cols = sketch // n
    parent = leaf_parent.T
    shape = jax.ShapeDtypeStruct
    held = pltpu.VMEM

    extra = rows + 2 * (b // n)
    fl, shared, *blocks = call(
        leaf_forward_kernel,
        "leaf_forward",
        (shape((leaf_count * b, sketch), BF), shape((all_rows, 2 * b), BF))
        + (held((extra, sketch), BF),) * n,
        [SMEM] * 2 + [VMEM] * 5,
        [pltpu.VMEM((all_rows + 2 * b, sketch), F32)],
        flops=2 * 12 * b * b * sketch,
        moved=4 << 20,
        limit=56,
    )(parent, row_owner, leaf_rhs, leaf_inv, leaf_coupling, sep_rhs, sep_inv)
    right, left = ring_sum(blocks)
    own = call(sum_own_kernel, "sum_own", held((extra, sketch), BF), [VMEM] * 3, moved=1 << 18)(
        near(right), near(left), near(blocks[0])
    )
    coupled = [near(block) for block in ring_gather(own)]

    shared = lax.psum_scatter(shared, "narrow", scatter_dimension=0, tiled=True)
    terms, maps = call(
        middle_kernel,
        "middle",
        (held((n, rows + cols + cols // 2, sketch), BF), held((3 * b, b), BF)),
        [SMEM] + [VMEM] * (2 + n) + [ANY],
        [pltpu.VMEM((all_rows, sketch), BF), pltpu.VMEM((b, b), F32), pltpu.VMEM((b, b), BF)],
        flops=4 * rows * all_rows * sketch,
        moved=4 << 20,
        limit=56,
    )(row_owner, sep_inv, *coupled, sep_link, shared)
    maps = call(stack_kernel, "stack_maps", held((4, 3 * b, b), BF), [VMEM] * 4, moved=1 << 18)(
        near(maps), *[near(turned_wide(maps, "x", k)) for k in (1, 2, 3)]
    )
    far, after, ahead = [turned_wide(maps, "y", k) for k in (2, 1, 3)]
    maps = [maps, after, far, ahead]
    maps_other = [swap(part, "wide", 1) for part in maps]

    terms = lax.all_to_all(terms, "narrow", 0, 0, tiled=True)
    terms = near(terms)
    ag = call(
        sum_ends_kernel,
        "sum_ends",
        held((chips, cols + cols // 2, 2 * b), BF),
        [VMEM],
        moved=1 << 19,
    )(terms)
    kept, packed = call(
        sum_terms_kernel,
        "sum_terms",
        (pltpu.HBM((rows, sketch), F32), pltpu.HBM((2 * rows, sketch), BF)),
        [VMEM] * 7,
        moved=2 << 20,
    )(terms, shared, near(ag), *[near(maps_other[j]) for j in (2, 0, 1)], near(maps[3]))
    gathered = lax.all_gather(packed, "narrow", axis=0, tiled=False)

    same_core = [[2 * q + c for q in range(chips)] for c in range(2)]
    ag = lax.all_to_all(ag, "wide", 0, 0, tiled=True, axis_index_groups=same_core)
    ag_other = near(swap(ag, "wide", 1))
    ag = near(ag)
    z = call(
        chain_kernel,
        "chain",
        held((n, cols, 2 * b), BF),
        [VMEM] * 2 + [ANY] * 7 + [VMEM] * 2,
        [
            pltpu.VMEM((2, chips, cols, 2 * b), F32),
            pltpu.VMEM((2, chips, 3 * b, b), BF),
            pltpu.VMEM((chain_len, cols, b), F32),
            pltpu.VMEM((chain_len, cols, b), F32),
            pltpu.SemaphoreType.DMA((2, chips)),
        ],
        flops=2 * 9 * chain_len * cols * b * b,
        moved=8 << 20,
        limit=56,
    )(ag, ag_other, *maps, *maps_other[:3], near(maps_other[3]), sep_link)
    z = lax.all_to_all(z, "narrow", 0, 0, tiled=True).reshape(sketch, 2 * b)

    base, fix, own = call(
        before_kernel,
        "before",
        (
            held((leaf_count * b, sketch), F32),
            held((leaf_count * b, 2 * b), BF),
            held((rows, 2 * b), BF),
        ),
        [SMEM] * 2 + [VMEM] * 3,
        flops=2 * 16 * b * b * sketch,
        moved=4 << 20,
        limit=56,
    )(parent, row_owner, gathered, leaf_coupling, fl)
    leaf_out, sep_out = call(
        final_kernel,
        "final",
        (shape((leaf_count * b, sketch), F32), shape((rows, sketch), F32)),
        [VMEM] * 6,
        flops=2 * 16 * b * b * sketch,
        moved=2 << 20,
    )(kept, near(own), near(base), near(fix), near(z), leaf_inv)
    return leaf_out, sep_out


def solution(mesh):
    both = ("wide", "narrow")
    placed = (
        P(both, None),
        P(both, None, None),
        P(both, None, None, None),
        P(both, None),
        P(both, None),
        P(both, None),
        P("wide", None),
        P("wide", None),
    )
    return jax.shard_map(
        per_device,
        mesh=mesh,
        in_specs=placed,
        out_specs=(P(both, None), P(both, None)),
        check_vma=False,
    )
```
